128 devices in a mesh: tile: 8 (over x, core), slab: 16 (over y, z).
Axes of the slice: x: 4, y: 4, z: 4, core: 2. Of those that a mesh axis runs over, the one named last changes fastest.
Arguments:
- pre_conv: bfloat16 [256, 32, 32, 512], P(('tile', 'slab')), may hold values from -6 to 6
- conv_weight: bfloat16 [4608, 1024], replicated, may hold values from -0.09375 to 0.09375
- proj_weight: bfloat16 [1024, 1280], replicated, may hold values from -0.1875 to 0.1875
- norm_gain: float32 [1280], replicated, may hold values from 0.25 to 1.75
- slab_cotangent: bfloat16 [131072, 1280], P(('tile', 'slab')), may hold values from -0.079589844 to 0.079589844
- page_tiles: int32 [128], P(('tile', 'slab')), may hold values from 1 to 2
- block_dest: int32 [1024, 1], P(('tile', 'slab')), may hold values from 0 to 15; in each aligned block of 8 rows (0 to 7, 8 to 15, ...) no two rows name the same one
Outputs:
- grad_conv: float32 [4608, 1024], P(('tile', 'slab'))
- grad_proj: float32 [1024, 1280], P(('tile', 'slab'))
- grad_gain: float32 [1280], replicated
The draws below stay inside these ranges and needn't reach their ends.
Inputs may be any that keep to these rules, and one draw needn't show every extreme that they name: The live tiles of a device are its first page_tiles ones. `block_dest`: the 8 blocks of one device name different slabs, so each slab receives at most one block from each device of its group.
All inputs are finite; a program needn't handle non-finite values.
Results may differ from the reference program's by a relative error of at most 0.0041.
Values may be sent and summed in bfloat16 or wider, within the bound.
No kernel may reach another device: no remote copies, remote signals or barrier semaphores. Data moves between devices by JAX's collectives and lax.ppermute only.
A program may use at most 128 MiB of HBM per device.

```python
import math
import jax
import jax.numpy as jnp
import numpy as np
from jax import lax

CIN = 512
COUT = 1024
DM = 1280
GRID = 32
TILES_DEV = 2
BLOCK_ROWS = 64
TOK_TILE = 256
BLK_DEV = 8
TILES = 256
BLOCKS = 1024
SLAB_ROWS = 131072
N_SLAB = 16
DEVICES = 128


def set_ends(drawn, stream_key, smallest, largest):
    extent = drawn.shape
    spot = [jax.random.randint(jax.random.fold_in(stream_key, axis), (), 0, extent[axis]) for axis in range(len(extent))]
    drawn = drawn.at[tuple(spot)].set(smallest)
    longest = extent.index(max(extent))
    spot[longest] = (spot[longest] + 1) % extent[longest]
    return drawn.at[tuple(spot)].set(largest)


def level_of(rng, shape, split, smallest, top_value):
    loudness = 1.0
    for axis_at, shards_of in split:
        heights = jax.random.uniform(jax.random.fold_in(jax.random.fold_in(rng, 6), axis_at), (shards_of,), jnp.float32, smallest / len(split), top_value / len(split))
        loudness = loudness * jnp.repeat(jnp.exp(heights), shape[axis_at] // shards_of).reshape((-1,) + (1,) * (len(shape) - 1 - axis_at))
    return loudness


def deal_out(own_key, own, number, rows, count, top, limit, slope):
    ranking = jax.random.permutation(own_key, count)
    packed, ordinary = shares(count, rows * top, limit, slope, True), shares(count, rows * top, limit, slope, False)
    places = jnp.arange(count)

    def named(tallies, offset_by):
        used = int((tallies > 0).sum())
        fixed = max(1, used // 4)
        passed = fixed + (places - fixed + offset_by * (used - fixed)) % max(1, count - fixed)
        return jnp.zeros((count,), jnp.int32).at[ranking[jnp.where(places < fixed, places, passed)]].set(jnp.asarray(tallies, jnp.int32))

    tallies = jnp.where(number % 4 == 0, named(packed, number // 4), named(ordinary, number - number // 4 - 1))
    mixed = jax.random.permutation(jax.random.fold_in(own, 3), count)
    donor, taker = mixed[0:count // 2 * 2:2], mixed[1:count // 2 * 2:2]
    slack = jnp.minimum(tallies[donor] - 1, limit - tallies[taker]) // 2
    slack = jnp.where((donor == ranking[0]) | (taker == ranking[0]) | (tallies[taker] == 0), 0, jnp.maximum(slack, 0))
    passed = jax.random.randint(jax.random.fold_in(own, 4), (count // 2,), 0, 1 << 20) % (slack + 1)
    tallies = tallies.at[donor].add(-passed).at[taker].add(passed)
    members = jnp.searchsorted(jnp.cumsum(tallies), jnp.arange(rows * top), side="right").astype(jnp.int32)
    grid = members.reshape(top, rows).T
    grid = grid[jax.random.permutation(jax.random.fold_in(own, 1), rows)]
    offset_by = jax.random.randint(jax.random.fold_in(own, 2), (rows, 1), 0, top)
    return jnp.take_along_axis(grid, (jnp.arange(top)[None, :] + offset_by) % top, axis=1)


def shares(amount, total, reach, slope, full):
    weights = [(1 << 20) // math.isqrt(grade ** slope) + 1 for grade in range(1, amount + 1)]
    largest = reach if full else min(reach, max(-(-total // amount), total * weights[0] // sum(weights)))
    least = 1 if total - largest >= amount - 1 else 0
    holding, surplus = [largest] + [least] * (amount - 1), total - largest - least * (amount - 1)
    while surplus > 0:
        free = [i for i in range(1, amount) if holding[i] < largest] or [i for i in range(1, amount) if holding[i] < reach]
        pool, remaining = sum([weights[i] for i in free]), surplus
        for i in free:
            extra = min(reach - holding[i], max(1, remaining * weights[i] // pool), surplus)
            holding[i] = holding[i] + extra
            surplus = surplus - extra
    return np.array(holding)


def normal_values(stream_key, dims, spread, bound, cuts=(), kind=jnp.bfloat16):
    array = jax.random.normal(stream_key, dims, jnp.float32) * spread
    if len(cuts) > 0:
        array = level_of(stream_key, dims, cuts, -0.22, 0.18) * array
    return jnp.clip(array, min=-bound, max=bound).astype(kind)


def setup_inputs(seed: int = 0) -> dict:
    seeds = jax.random.split(jax.random.key(seed), 8)
    pre_conv = normal_values(seeds[0], (TILES, GRID, GRID, CIN), 1.0, 6.0, ((0, 128),))
    conv_weight = normal_values(seeds[1], (9 * CIN, COUT), (9 * CIN) ** -0.5, 0.09375)
    proj_weight = normal_values(seeds[2], (COUT, DM), COUT ** -0.5, 0.1875)
    norm_gain = jnp.clip(1.0 + 0.15 * jax.random.normal(seeds[3], (DM,), jnp.float32), 0.25, 1.75)
    slab_cotangent = normal_values(seeds[4], (SLAB_ROWS, DM), 0.01, 0.079589844, ((0, 128),))
    page_tiles = set_ends(jax.random.randint(seeds[5], (DEVICES,), 1, TILES_DEV + 1), jax.random.fold_in(seeds[5], 1), 1, TILES_DEV).astype(jnp.int32)
    block_dest_keys = jax.random.split(jax.random.fold_in(seeds[6], 1), BLOCKS // BLK_DEV)
    block_dest_turns = jax.random.permutation(jax.random.fold_in(seeds[6], 3), BLOCKS // BLK_DEV)
    block_dest = jax.vmap(lambda own, number: deal_out(jax.random.fold_in(seeds[6], 2), own, number, BLK_DEV, N_SLAB, 1, 1, 2))(block_dest_keys, block_dest_turns).reshape((BLOCKS, 1))
    return dict(pre_conv=pre_conv, conv_weight=conv_weight, proj_weight=proj_weight, norm_gain=norm_gain, slab_cotangent=slab_cotangent, page_tiles=page_tiles, block_dest=block_dest)


epsilon = 1e-06

def patches(tile_input):
    grid_side = tile_input.shape[0]
    padded = jnp.pad(tile_input, ((1, 1), (1, 1), (0, 0)))
    pieces = [padded[row_off:row_off + grid_side:2, col_off:col_off + grid_side:2, :] for row_off in range(3) for col_off in range(3)]
    stacked = jnp.concatenate(pieces, axis=-1)
    return stacked.reshape(-1, stacked.shape[-1])

def reference(pre_conv, conv_weight, proj_weight, norm_gain, slab_cotangent, page_tiles, block_dest):
    tile_ids = jnp.arange(TILES, dtype=jnp.int32)
    is_live = tile_ids % TILES_DEV < page_tiles[tile_ids // TILES_DEV]

    def forward(tile_input):
        return jnp.dot(patches(tile_input), conv_weight, preferred_element_type=jnp.float32).astype(jnp.bfloat16)
    tokens = lax.map(forward, pre_conv)
    tokens = jnp.where(is_live[:, None, None], tokens, jnp.zeros_like(tokens))
    flat_tokens = tokens.reshape(-1, COUT)
    values = jnp.dot(flat_tokens, proj_weight, preferred_element_type=jnp.float32).reshape(BLOCKS, BLOCK_ROWS, DM)
    block_ids = jnp.arange(BLOCKS, dtype=jnp.int32)
    owner = block_ids // BLK_DEV
    landing = (owner // N_SLAB * N_SLAB + block_dest[:, 0]) * N_SLAB + owner % N_SLAB
    cotangent = slab_cotangent.reshape(-1, BLOCK_ROWS, DM)[landing].astype(jnp.float32)
    mean_square = lax.optimization_barrier(jnp.mean(values * values, axis=-1, keepdims=True))
    scale_inv = lax.rsqrt(mean_square + epsilon)
    upstream = cotangent * norm_gain
    inner = lax.optimization_barrier(jnp.mean(upstream * values, axis=-1, keepdims=True))
    grad_values = (scale_inv * upstream - values * scale_inv ** 3 * inner).astype(jnp.bfloat16)
    grad_gain = lax.optimization_barrier(jnp.sum(cotangent * values * scale_inv, axis=(0, 1)))
    flat_grads = grad_values.reshape(-1, DM)
    grad_proj = jnp.dot(flat_tokens.T, flat_grads, preferred_element_type=jnp.float32)
    grad_tokens = jnp.dot(flat_grads, proj_weight.T, preferred_element_type=jnp.float32).astype(jnp.bfloat16)
    grad_tokens = grad_tokens.reshape(TILES, TOK_TILE, COUT)
    grad_tokens = jnp.where(is_live[:, None, None], grad_tokens, jnp.zeros_like(grad_tokens))

    def accumulate(total, pair):
        tile_input, tile_grad = pair
        return (total + jnp.dot(patches(tile_input).T, tile_grad, preferred_element_type=jnp.float32), None)
    grad_conv, unused = lax.scan(accumulate, jnp.zeros((9 * CIN, COUT), jnp.float32), (pre_conv, grad_tokens))
    return (grad_conv, grad_proj, grad_gain)
```

```python
import functools

import jax
import jax.numpy as jnp
from jax import lax
from jax.experimental import pallas as pl
from jax.experimental.pallas import tpu as pltpu
from jax.sharding import Mesh
from jax.sharding import PartitionSpec as P

EPS = 1e-6
BF = jnp.bfloat16
F32 = jnp.float32
ALL = ("x", "core", "y", "z")
CHIPS = ("x", "y", "z")

CIN = 512
COUT = 1024
DM = 1280
TOK = 256
SIDE = 16
NX = 4
NYZ = 16
CONV_ROWS = 36
PROJ_ROWS = 8
XCONV = CONV_ROWS * NYZ
XPROJ = PROJ_ROWS * NYZ
XROWS = XCONV + XPROJ
CHUNK = 48


def dot(a, b, dims):
    return lax.dot_general(a, b, (dims, ((), ())), preferred_element_type=F32)


def selection():
    row = lax.broadcasted_iota(jnp.int32, (384, 256), 0)
    col = lax.broadcasted_iota(jnp.int32, (384, 256), 1)
    tap = lax.shift_right_logical(row, 7)
    parity = lax.shift_right_logical(row, 6) & 1
    y = lax.shift_right_logical(row, 4) & 3
    x = 2 * (row & 15) + tap - 1
    hit = (col == (2 * y + parity) * 32 + x) & (x >= 0)
    return jnp.where(hit, 1.0, 0.0)


def forward_kernel(
    core_ref, pages_ref, pre_ref, w_ref, proj_ref, own_ref, other_ref, values_ref, patch, patch_t, acc
):
    step = pl.program_id(0)

    @pl.when(step == 0)
    def _():
        select = selection()
        for t in range(2):
            live = jnp.where(t < pages_ref[0], 1.0, 0.0)
            chosen = (select * live).astype(BF)
            for c in range(3):
                patch[t * TOK : t * TOK + SIDE, c * CIN : (c + 1) * CIN] = jnp.zeros((SIDE, CIN), BF)
            for q in range(4):
                rows = pre_ref[t * 1024 + q * 256 : t * 1024 + (q + 1) * 256, :]
                got = dot(chosen, rows, ((1,), (0,))).astype(BF)
                at = t * TOK + q * 64
                for c in range(3):
                    even = got[c * 128 : c * 128 + 64]
                    odd = got[c * 128 + 64 : c * 128 + 128]
                    patch[at : at + 64, (3 + c) * CIN : (4 + c) * CIN] = even
                    patch[at : at + 64, (6 + c) * CIN : (7 + c) * CIN] = odd
                    if q < 3:
                        patch[at + 16 : at + 80, c * CIN : (c + 1) * CIN] = odd
                    else:
                        patch[at + 16 : at + 64, c * CIN : (c + 1) * CIN] = odd[:48]

    for k in range(9):

        @pl.when(step == k)
        def _(k=k):
            taps = patch[:, k * CIN : (k + 1) * CIN]
            part = dot(taps, w_ref[...], ((1,), (0,)))
            if k == 0:
                acc[...] = part
            else:
                acc[...] += part
            patch_t[k * CIN : (k + 1) * CIN, :] = taps.T

    @pl.when(step == 8)
    def _():
        tokens = acc[...].astype(BF)
        values_ref[...] = dot(tokens, proj_ref[...], ((1,), (0,)))
        patch_t[9 * CIN : 9 * CIN + COUT, :] = tokens.T
        core = core_ref[0]
        for x in range(NX):
            for who, ref in ((core, own_ref), (1 - core, other_ref)):
                a = 2 * x + who
                conv_at = pl.multiple_of(a * XCONV, 64)
                proj_at = pl.multiple_of(9 * CIN + a * XPROJ, 128)
                ref[x * XROWS : x * XROWS + XCONV, :] = patch_t[pl.ds(conv_at, XCONV), :]
                ref[x * XROWS + XCONV : (x + 1) * XROWS, :] = patch_t[pl.ds(proj_at, XPROJ), :]


def forward(core, pages, pre, w, proj):
    n = 2 * TOK
    smem = pl.BlockSpec(memory_space=pltpu.SMEM)
    return pl.pallas_call(
        forward_kernel,
        grid=(9,),
        in_specs=[
            smem,
            smem,
            pl.BlockSpec((2048, CIN), lambda k: (0, 0)),
            pl.BlockSpec((CIN, COUT), lambda k: (k, 0)),
            pl.BlockSpec((COUT, DM), lambda k: (0, 0)),
        ],
        out_specs=[
            pl.BlockSpec((NX * XROWS, n), lambda k: (0, 0)),
            pl.BlockSpec((NX * XROWS, n), lambda k: (0, 0)),
            pl.BlockSpec((n, DM), lambda k: (0, 0)),
        ],
        out_shape=[
            jax.ShapeDtypeStruct((NX * XROWS, n), BF),
            jax.ShapeDtypeStruct((NX * XROWS, n), BF),
            jax.ShapeDtypeStruct((n, DM), F32),
        ],
        scratch_shapes=[
            pltpu.VMEM((n, 9 * CIN), BF),
            pltpu.VMEM((9 * CIN + COUT, n), BF),
            pltpu.VMEM((n, COUT), F32),
        ],
        compiler_params=pltpu.CompilerParams(vmem_limit_bytes=56 << 20),
        cost_estimate=pl.CostEstimate(flops=6_200_000_000, bytes_accessed=24_000_000, transcendentals=0),
        name="forward",
    )(core, pages, pre, w, proj)


def norm_kernel(dest_ref, cot_ref, values_ref, gain_ref, grad_ref, gain_out_ref):
    step = pl.program_id(0)
    values = values_ref[...]
    cot = cot_ref[0].astype(F32)
    scale = lax.rsqrt(jnp.mean(values * values, axis=-1, keepdims=True) + EPS)
    up = cot * gain_ref[...]
    inner = jnp.mean(up * values, axis=-1, keepdims=True)
    grad_ref[...] = (scale * up - values * (scale * scale * scale * inner)).astype(BF)
    terms = jnp.sum(cot * values * scale, axis=0, keepdims=True)

    @pl.when(step == 0)
    def _():
        gain_out_ref[...] = jnp.zeros_like(gain_out_ref)

    gain_out_ref[...] += jnp.broadcast_to(terms, gain_out_ref.shape)


def norm(dest, cot, values, gain):
    return pl.pallas_call(
        norm_kernel,
        grid_spec=pltpu.PrefetchScalarGridSpec(
            num_scalar_prefetch=1,
            grid=(8,),
            in_specs=[
                pl.BlockSpec((1, 64, DM), lambda k, d: (d[k], 0, 0)),
                pl.BlockSpec((64, DM), lambda k, d: (k, 0)),
                pl.BlockSpec((1, DM), lambda k, d: (0, 0)),
            ],
            out_specs=[
                pl.BlockSpec((64, DM), lambda k, d: (k, 0)),
                pl.BlockSpec((8, DM), lambda k, d: (0, 0)),
            ],
        ),
        out_shape=[jax.ShapeDtypeStruct((512, DM), BF), jax.ShapeDtypeStruct((8, DM), F32)],
        compiler_params=pltpu.CompilerParams(vmem_limit_bytes=32 << 20),
        cost_estimate=pl.CostEstimate(flops=8_000_000, bytes_accessed=6_000_000, transcendentals=512),
        name="norm_backward",
    )(dest, cot, values, gain)


def backward_kernel(
    own_ref, other_ref, gown_ref, gother_ref, proj_ref, gain_own_ref, gain_other_ref, out_ref, gtok, conv, stage
):
    step = pl.program_id(0)

    @pl.when(step == 0)
    def _():
        gtok[:512] = dot(gown_ref[...], proj_ref[...], ((1,), (1,))).astype(BF)
        gtok[512:] = dot(gother_ref[...], proj_ref[...], ((1,), (1,))).astype(BF)

    conv[...] = dot(own_ref[:XCONV], gtok[:512], ((1,), (0,))) + dot(
        other_ref[:XCONV], gtok[512:], ((1,), (0,))
    )
    proj = dot(own_ref[XCONV:], gown_ref[...], ((1,), (0,))) + dot(
        other_ref[XCONV:], gother_ref[...], ((1,), (0,))
    )
    gain = gain_own_ref[0:1] + gain_other_ref[0:1]
    for k in range(NYZ):
        stage[0:8, :] = proj[8 * k : 8 * k + 8, :COUT]
        stage[8:44, :] = conv[36 * k : 36 * k + 36, :]
        for r in range(8):
            stage[44 + r // 4 : 45 + r // 4, (r % 4) * 256 : (r % 4 + 1) * 256] = proj[
                8 * k + r : 8 * k + r + 1, COUT:
            ]
        stage[46:47, :] = gain[:, :COUT]
        stage[47:48, :256] = gain[:, COUT:]
        stage[47:48, 256:] = jnp.zeros((1, COUT - 256), F32)
        out_ref[k] = stage[...].astype(BF)


def backward(own, other, gown, gother, proj, gain_own, gain_other):
    whole = lambda *s: pl.BlockSpec(s, lambda x: (0, 0))
    return pl.pallas_call(
        backward_kernel,
        grid=(NX,),
        in_specs=[
            pl.BlockSpec((XROWS, 512), lambda x: (x, 0)),
            pl.BlockSpec((XROWS, 512), lambda x: (x, 0)),
            whole(512, DM),
            whole(512, DM),
            whole(COUT, DM),
            whole(8, DM),
            whole(8, DM),
        ],
        out_specs=pl.BlockSpec((NYZ, CHUNK, COUT), lambda x: (x, 0, 0)),
        out_shape=jax.ShapeDtypeStruct((NX * NYZ, CHUNK, COUT), BF),
        scratch_shapes=[
            pltpu.VMEM((1024, COUT), BF),
            pltpu.VMEM((XCONV, COUT), F32),
            pltpu.VMEM((CHUNK, COUT), F32),
        ],
        compiler_params=pltpu.CompilerParams(vmem_limit_bytes=56 << 20),
        cost_estimate=pl.CostEstimate(flops=9_000_000_000, bytes_accessed=20_000_000, transcendentals=0),
        name="backward",
    )(own, other, gown, gother, proj, gain_own, gain_other)


def sum_kernel(got_ref, conv_ref, proj_ref, gain_ref, acc):
    step = pl.program_id(0)
    part = got_ref[0].astype(F32)
    for i in range(1, 8):
        part = part + got_ref[i].astype(F32)

    @pl.when(step == 0)
    def _():
        acc[...] = part

    @pl.when(step > 0)
    def _():
        acc[...] += part

    @pl.when(step == 7)
    def _():
        proj_ref[:, :COUT] = acc[0:8, :]
        conv_ref[...] = acc[8:44, :]
        for r in range(8):
            proj_ref[r : r + 1, COUT:] = acc[44 + r // 4 : 45 + r // 4, (r % 4) * 256 : (r % 4 + 1) * 256]
        gain_ref[:, :COUT] = acc[46:47, :]
        gain_ref[:, COUT:] = acc[47:48, :256]


def total(got):
    return pl.pallas_call(
        sum_kernel,
        grid=(8,),
        in_specs=[pl.BlockSpec((8, CHUNK, COUT), lambda k: (k, 0, 0))],
        out_specs=[
            pl.BlockSpec((CONV_ROWS, COUT), lambda k: (0, 0)),
            pl.BlockSpec((PROJ_ROWS, DM), lambda k: (0, 0)),
            pl.BlockSpec((1, DM), lambda k: (0, 0)),
        ],
        out_shape=[
            jax.ShapeDtypeStruct((CONV_ROWS, COUT), F32),
            jax.ShapeDtypeStruct((PROJ_ROWS, DM), F32),
            jax.ShapeDtypeStruct((1, DM), F32),
        ],
        scratch_shapes=[pltpu.VMEM((CHUNK, COUT), F32)],
        compiler_params=pltpu.CompilerParams(vmem_limit_bytes=32 << 20),
        cost_estimate=pl.CostEstimate(flops=3_000_000, bytes_accessed=6_500_000, transcendentals=0),
        name="total",
    )(got)


def per_device(pre_conv, conv_weight, proj_weight, norm_gain, slab_cotangent, page_tiles, block_dest):
    core = lax.axis_index("core").astype(jnp.int32).reshape(1)
    swap = functools.partial(lax.ppermute, axis_name="core", perm=[(0, 1), (1, 0)])
    cot = lax.all_to_all(slab_cotangent.reshape(16, 64, DM), ("y", "z"), 0, 0, tiled=True)
    own, other, values = forward(core, page_tiles, pre_conv.reshape(2048, CIN), conv_weight, proj_weight)
    other = swap(other)
    grads, gain = norm(block_dest[:, 0], cot, values, norm_gain.reshape(1, DM))
    chunks = backward(own, other, grads, swap(grads), proj_weight, gain, swap(gain))
    got = lax.all_to_all(chunks, CHIPS, 0, 0, tiled=True)
    grad_conv, grad_proj, grad_gain = total(got)
    return grad_conv, grad_proj, grad_gain.reshape(DM)


def solution(mesh):
    split = Mesh(mesh.devices.reshape(4, 2, 4, 4), ALL)
    return jax.shard_map(
        per_device,
        mesh=split,
        in_specs=(P(ALL), P(), P(), P(), P(ALL), P(ALL), P(ALL)),
        out_specs=(P(ALL), P(ALL), P()),
        check_vma=False,
    )
```

```python
import functools

import jax
import jax.numpy as jnp
from jax import lax
from jax.experimental import pallas as pl
from jax.experimental.pallas import tpu as pltpu
from jax.sharding import Mesh
from jax.sharding import PartitionSpec as P

EPS = 1e-6
BF = jnp.bfloat16
F32 = jnp.float32
ALL = ("x", "core", "y", "z")
CHIPS = ("x", "y", "z")

CIN = 512
COUT = 1024
DM = 1280
TOK = 256
SIDE = 16
NX = 4
NYZ = 16
CONV_ROWS = 36
PROJ_ROWS = 8
XCONV = CONV_ROWS * NYZ
XPROJ = PROJ_ROWS * NYZ
XROWS = XCONV + XPROJ
YROWS = XCONV // 4
HROWS = XCONV // 2
HALF = COUT // 2
LONG = 20_000_000_000


def dot(a, b, dims):
    return lax.dot_general(a, b, (dims, ((), ())), preferred_element_type=F32)


def selection():
    row = lax.broadcasted_iota(jnp.int32, (384, 256), 0)
    col = lax.broadcasted_iota(jnp.int32, (384, 256), 1)
    tap = lax.shift_right_logical(row, 7)
    parity = lax.shift_right_logical(row, 6) & 1
    y = lax.shift_right_logical(row, 4) & 3
    x = 2 * (row & 15) + tap - 1
    hit = (col == (2 * y + parity) * 32 + x) & (x >= 0)
    return jnp.where(hit, 1.0, 0.0)


def forward_kernel(
    core_ref, pages_ref, pre_ref, w_ref, proj_ref, own_ref, other_ref, values_ref, proj_t_ref, patch, patch_t, acc
):
    step = pl.program_id(0)

    @pl.when(step == 0)
    def _():
        select = selection()
        for t in range(2):
            live = jnp.where(t < pages_ref[0], 1.0, 0.0)
            chosen = (select * live).astype(BF)
            for c in range(3):
                patch[t * TOK : t * TOK + SIDE, c * CIN : (c + 1) * CIN] = jnp.zeros((SIDE, CIN), BF)
            for q in range(4):
                rows = pre_ref[t * 1024 + q * 256 : t * 1024 + (q + 1) * 256, :]
                got = dot(chosen, rows, ((1,), (0,))).astype(BF)
                at = t * TOK + q * 64
                for c in range(3):
                    even = got[c * 128 : c * 128 + 64]
                    odd = got[c * 128 + 64 : c * 128 + 128]
                    patch[at : at + 64, (3 + c) * CIN : (4 + c) * CIN] = even
                    patch[at : at + 64, (6 + c) * CIN : (7 + c) * CIN] = odd
                    if q < 3:
                        patch[at + 16 : at + 80, c * CIN : (c + 1) * CIN] = odd
                    else:
                        patch[at + 16 : at + 64, c * CIN : (c + 1) * CIN] = odd[:48]

    for k in range(9):

        @pl.when(step == k)
        def _(k=k):
            taps = patch[:, k * CIN : (k + 1) * CIN]
            part = dot(taps, w_ref[...], ((1,), (0,)))
            if k == 0:
                acc[...] = part
            else:
                acc[...] += part
            patch_t[k * CIN : (k + 1) * CIN, :] = taps.T

    @pl.when(step == 8)
    def _():
        tokens = acc[...].astype(BF)
        values_ref[...] = dot(tokens, proj_ref[...], ((1,), (0,)))
        proj_t_ref[...] = proj_ref[...].T
        patch_t[9 * CIN : 9 * CIN + COUT, :] = tokens.T
        core = core_ref[1]
        for x in range(NX):
            for who, ref in ((core, own_ref), (1 - core, other_ref)):
                a = 2 * x + who
                conv_at = pl.multiple_of(a * XCONV, 64)
                proj_at = pl.multiple_of(9 * CIN + a * XPROJ, 128)
                ref[x * XCONV : (x + 1) * XCONV, :] = patch_t[pl.ds(conv_at, XCONV), :]
                to = NX * XCONV + x * XPROJ
                ref[to : to + XPROJ, :] = patch_t[pl.ds(proj_at, XPROJ), :]


def forward(core, pages, pre, w, proj):
    n = 2 * TOK
    smem = pl.BlockSpec(memory_space=pltpu.SMEM)
    return pl.pallas_call(
        forward_kernel,
        grid=(9,),
        in_specs=[
            smem,
            smem,
            pl.BlockSpec((2048, CIN), lambda k: (0, 0)),
            pl.BlockSpec((CIN, COUT), lambda k: (k, 0)),
            pl.BlockSpec((COUT, DM), lambda k: (0, 0)),
        ],
        out_specs=[
            pl.BlockSpec((NX * XROWS, n), lambda k: (0, 0)),
            pl.BlockSpec((NX * XROWS, n), lambda k: (0, 0)),
            pl.BlockSpec((n, DM), lambda k: (0, 0)),
            pl.BlockSpec((DM, COUT), lambda k: (0, 0)),
        ],
        out_shape=[
            jax.ShapeDtypeStruct((NX * XROWS, n), BF),
            jax.ShapeDtypeStruct((NX * XROWS, n), BF),
            jax.ShapeDtypeStruct((n, DM), F32),
            jax.ShapeDtypeStruct((DM, COUT), BF),
        ],
        scratch_shapes=[
            pltpu.VMEM((n, 9 * CIN), BF),
            pltpu.VMEM((9 * CIN + COUT, n), BF),
            pltpu.VMEM((n, COUT), F32),
        ],
        compiler_params=pltpu.CompilerParams(vmem_limit_bytes=60 << 20),
        cost_estimate=pl.CostEstimate(flops=6_200_000_000, bytes_accessed=24_000_000, transcendentals=0),
        name="forward",
    )(core, pages, pre, w, proj)


def norm_kernel(
    dest_ref, cot_ref, values_hbm, gain_ref, proj_t_hbm, grad_ref, gain_out_ref, proj_t_ref, values, sems
):
    copies = [pltpu.make_async_copy(values_hbm.at[k], values.at[k], sems.at[k]) for k in range(8)]
    copies.append(pltpu.make_async_copy(proj_t_hbm, proj_t_ref, sems.at[8]))
    for copy in copies:
        copy.start()
    total = jnp.zeros((8, DM), F32)
    for k in range(8):
        c = cot_ref[dest_ref[k]].astype(F32)
        copies[k].wait()
        v = values[k]
        scale = lax.rsqrt(jnp.mean(v * v, axis=-1, keepdims=True) + EPS)
        up = c * gain_ref[...]
        inner = jnp.mean(up * v, axis=-1, keepdims=True)
        grad_ref[64 * k : 64 * k + 64, :] = (scale * up - v * (scale * scale * scale * inner)).astype(BF)
        total = total + jnp.sum((c * v * scale).reshape(8, 8, DM), axis=0)
    gain_out_ref[...] = jnp.broadcast_to(jnp.sum(total, axis=0, keepdims=True), (8, DM))
    copies[8].wait()


SMEM_SPEC = pl.BlockSpec(memory_space=pltpu.SMEM)
VMEM_SPEC = pl.BlockSpec(memory_space=pltpu.VMEM)
HBM_SPEC = pl.BlockSpec(memory_space=pltpu.HBM)
ANY_SPEC = pl.BlockSpec(memory_space=pl.ANY)


def in_hbm(array):
    return pltpu.with_memory_space_constraint(array, pltpu.HBM)


def norm(dest, cot, values, gain, proj_t):
    return pl.pallas_call(
        norm_kernel,
        in_specs=[SMEM_SPEC, VMEM_SPEC, HBM_SPEC, VMEM_SPEC, HBM_SPEC],
        out_specs=[VMEM_SPEC] * 3,
        out_shape=[
            jax.ShapeDtypeStruct((512, DM), BF),
            jax.ShapeDtypeStruct((8, DM), F32),
            pltpu.VMEM((DM, COUT), BF),
        ],
        scratch_shapes=[pltpu.VMEM((8, 64, DM), F32), pltpu.SemaphoreType.DMA((9,))],
        compiler_params=pltpu.CompilerParams(vmem_limit_bytes=16 << 20),
        cost_estimate=pl.CostEstimate(flops=8_000_000, bytes_accessed=8_000_000, transcendentals=512),
        name="norm_backward",
    )(dest, cot, in_hbm(values.reshape(8, 64, DM)), gain, in_hbm(proj_t))


def token_kernel(
    grad_ref, proj_t_ref, own_hbm, other_hbm, out_ref, own_ref, other_ref, own_tok_ref, other_tok_ref, sems
):
    copies = []
    for x in range(4):
        rows = pl.ds(x * XCONV, XCONV)
        copies.append(pltpu.make_async_copy(own_hbm.at[rows], own_ref.at[x], sems.at[0, x]))
        copies.append(pltpu.make_async_copy(other_hbm.at[rows], other_ref.at[x], sems.at[1, x]))
    rows = pl.ds(NX * XCONV, NX * XPROJ)
    copies.append(pltpu.make_async_copy(own_hbm.at[rows], own_tok_ref, sems.at[0, 4]))
    copies.append(pltpu.make_async_copy(other_hbm.at[rows], other_tok_ref, sems.at[1, 4]))
    for copy in copies:
        copy.start()
    out_ref[...] = dot(grad_ref[...], proj_t_ref[...], ((1,), (0,))).astype(BF)
    for copy in copies:
        copy.wait()


def token_grad(grads, proj_t, own, other):
    return pl.pallas_call(
        token_kernel,
        in_specs=[VMEM_SPEC, VMEM_SPEC, HBM_SPEC, HBM_SPEC],
        out_specs=[VMEM_SPEC] * 5,
        out_shape=[jax.ShapeDtypeStruct((512, COUT), BF)]
        + [pltpu.VMEM((NX, XCONV, 512), BF)] * 2
        + [pltpu.VMEM((NX * XPROJ, 512), BF)] * 2,
        scratch_shapes=[pltpu.SemaphoreType.DMA((2, 5))],
        compiler_params=pltpu.CompilerParams(vmem_limit_bytes=16 << 20),
        cost_estimate=pl.CostEstimate(flops=1_340_000_000, bytes_accessed=8_000_000, transcendentals=0),
        name="token_grad",
    )(grads, proj_t, in_hbm(own), in_hbm(other))


def by_turn(axis, pos_ref, s, rows_ref):
    if axis == 0:
        return rows_ref[(pos_ref[0] + s) & 3]
    rows = pl.ds(pl.multiple_of(((pos_ref[2] + s) & 3) * YROWS, 16), YROWS)
    return jnp.concatenate([rows_ref[x, rows, :] for x in range(NX)], axis=0)


def conv_block(axis, pos_ref, s, own, other, gtok, gtok_other):
    at = pl.ds(axis * HALF // 2, HALF)
    return (
        dot(by_turn(axis, pos_ref, s, own), gtok[:, at], ((1,), (0,)))
        + dot(by_turn(axis, pos_ref, s, other), gtok_other[:, at], ((1,), (0,)))
    ).astype(BF)


def conv_first_kernel(pos_ref, own, other, gtok, gother, proj_t, after, *rest):
    outs, gtok_other, part, sems = rest[:4], rest[4], rest[5], rest[6]
    gtok_other[...] = dot(gother[...], proj_t[...], ((1,), (0,))).astype(BF)
    sends = []
    for slot, axis in enumerate((0, 2)):
        part[slot] = conv_block(axis, pos_ref, 2, own, other, gtok, gtok_other)
        for half in range(2):
            rows = part.at[slot, pl.ds(half * HROWS, HROWS)]
            sends.append(pltpu.make_async_copy(rows, outs[2 * slot + half], sems.at[slot, half]))
            sends[-1].start()
    for copy in sends:
        copy.wait()


def conv_first(pos, own, other, gtok, gother, proj_t, after):
    return pl.pallas_call(
        conv_first_kernel,
        in_specs=[SMEM_SPEC] + [VMEM_SPEC] * 5 + [ANY_SPEC],
        out_specs=[HBM_SPEC] * 4 + [VMEM_SPEC],
        out_shape=[pltpu.HBM((HROWS, HALF), BF)] * 4 + [jax.ShapeDtypeStruct((512, COUT), BF)],
        scratch_shapes=[pltpu.VMEM((2, XCONV, HALF), BF), pltpu.SemaphoreType.DMA((2, 2))],
        compiler_params=pltpu.CompilerParams(vmem_limit_bytes=16 << 20),
        cost_estimate=pl.CostEstimate(flops=2_500_000_000, bytes_accessed=2_000_000, transcendentals=0),
        name="conv_first",
    )(pos, own, other, gtok, gother, proj_t, after)


def conv_second_kernel(pos_ref, own, other, gtok, gtok_other, through_in, *rest):
    outs, through_out, part, sems = rest[:6], rest[6], rest[7], rest[8]
    sends = []
    for axis in (0, 2):
        for s in (1, 3, 0):
            slot = len(sends)
            part[slot] = conv_block(axis, pos_ref, s, own, other, gtok, gtok_other)
            sends.append(pltpu.make_async_copy(part.at[slot], outs[slot], sems.at[slot]))
            sends[-1].start()
    for copy in sends:
        copy.wait()


def conv_second(pos, own, other, gtok, gtok_other, through):
    return pl.pallas_call(
        conv_second_kernel,
        in_specs=[SMEM_SPEC] + [VMEM_SPEC] * 4 + [HBM_SPEC],
        out_specs=[HBM_SPEC] * 7,
        out_shape=[pltpu.HBM((XCONV, HALF), BF)] * 6 + [pltpu.HBM(through.shape, through.dtype)],
        input_output_aliases={5: 6},
        scratch_shapes=[pltpu.VMEM((6, XCONV, HALF), BF), pltpu.SemaphoreType.DMA((6,))],
        compiler_params=pltpu.CompilerParams(vmem_limit_bytes=16 << 20),
        cost_estimate=pl.CostEstimate(flops=3_700_000_000, bytes_accessed=3_000_000, transcendentals=0),
        name="conv_second",
    )(pos, own, other, gtok, gtok_other, in_hbm(through))


def add_kernel(ahead_in, behind_in, from_behind, from_ahead, ahead, behind, part, sems):
    halves = (
        (ahead_in, ahead, pl.ds(0, HROWS), from_behind),
        (behind_in, behind, pl.ds(HROWS, HROWS), from_ahead),
    )
    loads = [
        pltpu.make_async_copy(old.at[rows], part.at[i], sems.at[0, i]) for i, (old, _, rows, _) in enumerate(halves)
    ]
    stores = [
        pltpu.make_async_copy(part.at[i], new.at[rows], sems.at[1, i]) for i, (_, new, rows, _) in enumerate(halves)
    ]
    for copy in loads:
        copy.start()
    for i in range(2):
        loads[i].wait()
        part[i] = (part[i].astype(F32) + halves[i][3][...].astype(F32)).astype(BF)
        stores[i].start()
    for copy in stores:
        copy.wait()


def relay(axis, halves, ahead, behind, here):
    forward, back = [(i, (i + 1) % 4) for i in range(4)], [(i, (i + 3) % 4) for i in range(4)]
    from_behind = lax.ppermute(halves[0], axis, forward)
    from_ahead = lax.ppermute(halves[1], axis, back)

    def finish():
        one, other = pl.pallas_call(
            add_kernel,
            in_specs=[HBM_SPEC, HBM_SPEC, VMEM_SPEC, VMEM_SPEC],
            out_specs=[HBM_SPEC] * 2,
            out_shape=[pltpu.HBM((XCONV, HALF), BF)] * 2,
            input_output_aliases={0: 0, 1: 1},
            scratch_shapes=[pltpu.VMEM((2, HROWS, HALF), BF), pltpu.SemaphoreType.DMA((2, 2))],
            compiler_params=pltpu.CompilerParams(vmem_limit_bytes=16 << 20),
            cost_estimate=pl.CostEstimate(flops=LONG, bytes_accessed=3_000_000, transcendentals=0),
            name="add_" + axis,
        )(in_hbm(ahead), in_hbm(behind), from_behind, from_ahead)
        return [here, lax.ppermute(one, axis, forward), lax.ppermute(other, axis, back)]

    return finish()


def split_gain(gain):
    high = gain.astype(BF).astype(F32)
    rest = gain - high
    low = rest.astype(BF).astype(F32)
    return jnp.concatenate(
        [
            jnp.broadcast_to(high, (8, DM)),
            jnp.broadcast_to(low, (8, DM)),
        ],
        axis=0,
    )


def proj_kernel(own, other, gown, gother, gain_own, gain_other, after, out_hbm, part, out, sem):
    gain = split_gain(gain_own[0:1] + gain_other[0:1]).astype(BF)
    for z in range(4):
        out[z, 128:144, :] = gain
    for x in range(4):
        rows = slice(x * XPROJ, (x + 1) * XPROJ)
        part[...] = dot(own[rows, :], gown[...], ((1,), (0,))) + dot(other[rows, :], gother[...], ((1,), (0,)))
        for z in range(4):
            pick = [part[y * 32 + z * 8 : y * 32 + z * 8 + 8, :] for y in range(4)]
            out[z, x * 32 : x * 32 + 32, :] = jnp.concatenate(pick, axis=0).astype(BF)
    copy = pltpu.make_async_copy(out, out_hbm, sem)
    copy.start()
    copy.wait()


def proj_grad(own, other, gown, gother, gain_own, gain_other, after):
    return pl.pallas_call(
        proj_kernel,
        in_specs=[VMEM_SPEC] * 6 + [ANY_SPEC],
        out_specs=HBM_SPEC,
        out_shape=pltpu.HBM((4, 144, DM), BF),
        scratch_shapes=[
            pltpu.VMEM((XPROJ, DM), F32),
            pltpu.VMEM((4, 144, DM), BF),
            pltpu.SemaphoreType.DMA,
        ],
        compiler_params=pltpu.CompilerParams(vmem_limit_bytes=16 << 20),
        cost_estimate=pl.CostEstimate(flops=1_400_000_000, bytes_accessed=2_000_000, transcendentals=0),
        name="proj_grad",
    )(own, other, gown, gother, gain_own, gain_other, after)


def small(kernel, name, outs, args, scratch=(), mib=16, flops=1_000_000, after=()):
    bytes_in = sum(a.size * a.dtype.itemsize for a in args)
    return pl.pallas_call(
        kernel,
        in_specs=[SMEM_SPEC] + [VMEM_SPEC] * (len(args) - 1) + [ANY_SPEC] * len(after),
        out_specs=[VMEM_SPEC] * len(outs),
        out_shape=[jax.ShapeDtypeStruct(*o) for o in outs],
        scratch_shapes=list(scratch),
        compiler_params=pltpu.CompilerParams(vmem_limit_bytes=mib << 20),
        cost_estimate=pl.CostEstimate(flops=flops, bytes_accessed=bytes_in, transcendentals=0),
        name=name,
    )(*args, *after)


def first_sum_kernel(pos_ref, a, b, c, *outs):
    for s, ref in enumerate(outs):
        at = pl.ds(pl.multiple_of(((pos_ref[2] + s) & 3) * YROWS, 16), YROWS)
        ref[...] = (a[at, :].astype(F32) + (b[at, :].astype(F32) + c[at, :].astype(F32))).astype(BF)


def second_sum_kernel(pos_ref, a, b, c, proj_ref, *outs):
    gains = [proj_ref[i, 128:136, :].astype(F32) + proj_ref[i, 136:144, :].astype(F32) for i in range(4)]
    gain = split_gain(((gains[0] + gains[1]) + (gains[2] + gains[3]))[0:1])
    for s, ref in enumerate(outs):
        x = (pos_ref[0] + s) & 3
        at = pl.ds(pl.multiple_of(x * YROWS, 16), YROWS)
        ref[0:YROWS, :] = (a[at, :].astype(F32) + (b[at, :].astype(F32) + c[at, :].astype(F32))).astype(BF)
        at = pl.ds(pl.multiple_of(x * 32, 32), 32)
        rows = [proj_ref[i, at, :].astype(F32) for i in range(4)]
        rows = (rows[0] + rows[1]) + (rows[2] + rows[3])
        rows = jnp.concatenate([rows, gain], axis=0).astype(BF)
        ref[144:192, :] = rows[:, :512]
        ref[192:240, :] = rows[:, 512:1024]
        ref[240:288, 0:256] = rows[:, 1024:]
        ref[240:288, 256:512] = jnp.zeros((48, 256), BF)


def plane_sum_kernel(pos_ref, a0, a1, a2, a3, b0, b1, b2, b3, o0, o1, o2, o3, part, by_z):
    for at, refs in ((0, (a0, a1, a2, a3)), (HALF, (b0, b1, b2, b3))):
        p, q, r, t = [ref[0:YROWS, :].astype(F32) for ref in refs]
        part[:, at : at + HALF] = (p + q) + (r + t)
    for z in range(4):
        by_z[z, 0:36, :] = part[36 * z : 36 * z + 36, :]
    for s, ref in enumerate((o0, o1, o2, o3)):
        ref[...] = by_z[(pos_ref[3] + s) & 3, 0:36, :].astype(BF)


def conv_total_kernel(pos_ref, a, b, c, d, out_ref):
    out_ref[...] = (a[...].astype(F32) + b[...].astype(F32)) + (c[...].astype(F32) + d[...].astype(F32))


def proj_plane_kernel(pos_ref, a, b, c, d, out_ref, gains, part):
    rows = []
    for s, ref in enumerate((a, b, c, d)):
        got = jnp.concatenate(
            [ref[144:192, :], ref[192:240, :], ref[240:288, 0:256]], axis=1
        ).astype(F32)
        rows.append(got[0:32])
        gains[(pos_ref[0] - s) & 3] = got[32:40] + got[40:48]
    part[...] = (rows[0] + rows[1]) + (rows[2] + rows[3])
    gain = split_gain(((gains[0] + gains[1]) + (gains[2] + gains[3]))[0:1])
    gain = jnp.concatenate([gain[0:4], gain[8:12]], axis=0)
    for y in range(4):
        out_ref[y] = jnp.concatenate([part[8 * y : 8 * y + 8, :], gain], axis=0).astype(BF)


def proj_total_kernel(pos_ref, got_ref, out_ref, gain_ref):
    got = [got_ref[i].astype(F32) for i in range(4)]
    total = (got[0] + got[1]) + (got[2] + got[3])
    out_ref[...] = total[0:8]
    gain_ref[...] = total[8:9] + total[12:13]


def turn(axis, parts):
    return [parts[0]] + [
        lax.ppermute(parts[s], axis, [(i, (i + s) % 4) for i in range(4)]) for s in (1, 2, 3)
    ]


def per_device(pre_conv, conv_weight, proj_weight, norm_gain, slab_cotangent, page_tiles, block_dest):
    pos = jnp.stack([lax.axis_index(axis) for axis in ALL]).astype(jnp.int32)
    swap = functools.partial(lax.ppermute, axis_name="core", perm=[(0, 1), (1, 0)])
    cot = lax.all_to_all(slab_cotangent.reshape(16, 64, DM), ("y", "z"), 0, 0, tiled=True)
    own, other, values, proj_t = forward(
        pos, page_tiles, pre_conv.reshape(2048, CIN), conv_weight, proj_weight
    )
    other = swap(other)
    grads, gain, proj_t = norm(block_dest[:, 0], cot, values, norm_gain.reshape(1, DM), proj_t)
    gother, gain_other = swap(grads), swap(gain)

    gtok, mine, theirs, my_tokens, their_tokens = token_grad(grads, proj_t, own, other)
    *halves, gtok_other = conv_first(pos, mine, theirs, gtok, gother, proj_t, gain_other)
    proj = proj_grad(my_tokens, their_tokens, grads, gother, gain, gain_other, gtok_other)
    *shares, proj = conv_second(pos, mine, theirs, gtok, gtok_other, proj)
    proj = lax.all_to_all(proj, "z", 0, 0, tiled=True)
    first = relay("x", halves[:2], *shares[:3])
    second = relay("y", halves[2:], *shares[3:])

    plane = ((YROWS, HALF), BF)
    wide = ((2 * YROWS, HALF), BF)
    first = turn("y", small(first_sum_kernel, "first_sum", [plane] * 4, [pos, *first], flops=LONG))
    second = turn("x", small(second_sum_kernel, "second_sum", [wide] * 4, [pos, *second, proj], flops=LONG))
    (proj,) = small(
        proj_plane_kernel,
        "proj_plane",
        [((4, 16, DM), BF)],
        [pos, *second],
        [pltpu.VMEM((4, 8, DM), F32), pltpu.VMEM((32, DM), F32)],
    )
    proj = lax.all_to_all(proj, "y", 0, 0, tiled=True)
    grad_proj, grad_gain = small(
        proj_total_kernel, "proj_total", [((PROJ_ROWS, DM), F32), ((1, DM), F32)], [pos, proj]
    )
    both = small(
        plane_sum_kernel,
        "plane_sum",
        [((CONV_ROWS, COUT), BF)] * 4,
        [pos, *first, *second],
        [pltpu.VMEM((YROWS, COUT), F32), pltpu.VMEM((4, 40, COUT), F32)],
        flops=LONG,
    )
    (grad_conv,) = small(
        conv_total_kernel,
        "conv_total",
        [((CONV_ROWS, COUT), F32)],
        [pos, *turn("z", both)],
        flops=LONG,
    )
    return grad_conv, grad_proj, grad_gain.reshape(DM)


def solution(mesh):
    split = Mesh(mesh.devices.reshape(4, 2, 4, 4), ALL)
    return jax.shard_map(
        per_device,
        mesh=split,
        in_specs=(P(ALL), P(), P(), P(), P(ALL), P(ALL), P(ALL)),
        out_specs=(P(ALL), P(ALL), P()),
        check_vma=False,
    )
```

```python
import functools

import jax
import jax.numpy as jnp
from jax import lax
from jax.experimental import pallas as pl
from jax.experimental.pallas import tpu as pltpu
from jax.sharding import Mesh
from jax.sharding import PartitionSpec as P

EPS = 1e-6
BF = jnp.bfloat16
F32 = jnp.float32
ALL = ("x", "core", "y", "z")
CHIPS = ("x", "y", "z")

CIN = 512
COUT = 1024
DM = 1280
TOK = 256
SIDE = 16
NX = 4
NYZ = 16
CONV_ROWS = 36
PROJ_ROWS = 8
XCONV = CONV_ROWS * NYZ
XPROJ = PROJ_ROWS * NYZ
XROWS = XCONV + XPROJ
YROWS = XCONV // 4
HROWS = XCONV // 2
HALF = COUT // 2
COST_ADD = 1
COST_SUM = 1
COST_PROJ = 20000000000
COST_SECOND = 20000000000


def dot(a, b, dims):
    return lax.dot_general(a, b, (dims, ((), ())), preferred_element_type=F32)


def selection():
    row = lax.broadcasted_iota(jnp.int32, (384, 256), 0)
    col = lax.broadcasted_iota(jnp.int32, (384, 256), 1)
    tap = lax.shift_right_logical(row, 7)
    parity = lax.shift_right_logical(row, 6) & 1
    y = lax.shift_right_logical(row, 4) & 3
    x = 2 * (row & 15) + tap - 1
    hit = (col == (2 * y + parity) * 32 + x) & (x >= 0)
    return jnp.where(hit, 1.0, 0.0)


def forward_kernel(
    core_ref, pages_ref, pre_ref, w_ref, proj_ref, own_ref, other_ref, values_ref, proj_t_ref, patch, patch_t, acc
):
    step = pl.program_id(0)

    @pl.when(step == 0)
    def _():
        select = selection()
        for t in range(2):
            live = jnp.where(t < pages_ref[0], 1.0, 0.0)
            chosen = (select * live).astype(BF)
            for c in range(3):
                patch[t * TOK : t * TOK + SIDE, c * CIN : (c + 1) * CIN] = jnp.zeros((SIDE, CIN), BF)
            for q in range(4):
                rows = pre_ref[t * 1024 + q * 256 : t * 1024 + (q + 1) * 256, :]
                got = dot(chosen, rows, ((1,), (0,))).astype(BF)
                at = t * TOK + q * 64
                for c in range(3):
                    even = got[c * 128 : c * 128 + 64]
                    odd = got[c * 128 + 64 : c * 128 + 128]
                    patch[at : at + 64, (3 + c) * CIN : (4 + c) * CIN] = even
                    patch[at : at + 64, (6 + c) * CIN : (7 + c) * CIN] = odd
                    if q < 3:
                        patch[at + 16 : at + 80, c * CIN : (c + 1) * CIN] = odd
                    else:
                        patch[at + 16 : at + 64, c * CIN : (c + 1) * CIN] = odd[:48]

    for k in range(9):

        @pl.when(step == k)
        def _(k=k):
            taps = patch[:, k * CIN : (k + 1) * CIN]
            part = dot(taps, w_ref[...], ((1,), (0,)))
            if k == 0:
                acc[...] = part
            else:
                acc[...] += part
            patch_t[k * CIN : (k + 1) * CIN, :] = taps.T

    @pl.when(step == 8)
    def _():
        tokens = acc[...].astype(BF)
        values_ref[...] = dot(tokens, proj_ref[...], ((1,), (0,)))
        proj_t_ref[...] = proj_ref[...].T
        patch_t[9 * CIN : 9 * CIN + COUT, :] = tokens.T
        core = core_ref[1]
        for x in range(NX):
            for who, ref in ((core, own_ref), (1 - core, other_ref)):
                a = 2 * x + who
                conv_at = pl.multiple_of(a * XCONV, 64)
                proj_at = pl.multiple_of(9 * CIN + a * XPROJ, 128)
                ref[x * XCONV : (x + 1) * XCONV, :] = patch_t[pl.ds(conv_at, XCONV), :]
                to = NX * XCONV + x * XPROJ
                ref[to : to + XPROJ, :] = patch_t[pl.ds(proj_at, XPROJ), :]


def forward(core, pages, pre, w, proj):
    n = 2 * TOK
    smem = pl.BlockSpec(memory_space=pltpu.SMEM)
    return pl.pallas_call(
        forward_kernel,
        grid=(9,),
        in_specs=[
            smem,
            smem,
            pl.BlockSpec((2048, CIN), lambda k: (0, 0)),
            pl.BlockSpec((CIN, COUT), lambda k: (k, 0)),
            pl.BlockSpec((COUT, DM), lambda k: (0, 0)),
        ],
        out_specs=[
            pl.BlockSpec((NX * XROWS, n), lambda k: (0, 0)),
            pl.BlockSpec((NX * XROWS, n), lambda k: (0, 0)),
            pl.BlockSpec((n, DM), lambda k: (0, 0)),
            pl.BlockSpec((DM, COUT), lambda k: (0, 0)),
        ],
        out_shape=[
            jax.ShapeDtypeStruct((NX * XROWS, n), BF),
            jax.ShapeDtypeStruct((NX * XROWS, n), BF),
            jax.ShapeDtypeStruct((n, DM), F32),
            jax.ShapeDtypeStruct((DM, COUT), BF),
        ],
        scratch_shapes=[
            pltpu.VMEM((n, 9 * CIN), BF),
            pltpu.VMEM((9 * CIN + COUT, n), BF),
            pltpu.VMEM((n, COUT), F32),
        ],
        compiler_params=pltpu.CompilerParams(vmem_limit_bytes=60 << 20),
        cost_estimate=pl.CostEstimate(flops=6_200_000_000, bytes_accessed=24_000_000, transcendentals=0),
        name="forward",
    )(core, pages, pre, w, proj)


def norm_kernel(
    dest_ref, cot_ref, values_hbm, gain_ref, proj_t_hbm, grad_ref, gain_out_ref, proj_t_ref, values, sems
):
    copies = [pltpu.make_async_copy(values_hbm.at[k], values.at[k], sems.at[k]) for k in range(8)]
    copies.append(pltpu.make_async_copy(proj_t_hbm.at[:, pl.ds(0, HALF)], proj_t_ref, sems.at[8]))
    for copy in copies:
        copy.start()
    total = jnp.zeros((8, DM), F32)
    for k in range(8):
        c = cot_ref[dest_ref[k]].astype(F32)
        copies[k].wait()
        v = values[k]
        scale = lax.rsqrt(jnp.mean(v * v, axis=-1, keepdims=True) + EPS)
        up = c * gain_ref[...]
        inner = jnp.mean(up * v, axis=-1, keepdims=True)
        grad_ref[64 * k : 64 * k + 64, :] = (scale * up - v * (scale * scale * scale * inner)).astype(BF)
        total = total + jnp.sum((c * v * scale).reshape(8, 8, DM), axis=0)
    gain_out_ref[...] = jnp.broadcast_to(jnp.sum(total, axis=0, keepdims=True), (8, DM))
    copies[8].wait()


SMEM_SPEC = pl.BlockSpec(memory_space=pltpu.SMEM)
VMEM_SPEC = pl.BlockSpec(memory_space=pltpu.VMEM)
HBM_SPEC = pl.BlockSpec(memory_space=pltpu.HBM)
ANY_SPEC = pl.BlockSpec(memory_space=pl.ANY)


def in_hbm(array):
    return pltpu.with_memory_space_constraint(array, pltpu.HBM)


def norm(dest, cot, values, gain, proj_t):
    return pl.pallas_call(
        norm_kernel,
        in_specs=[SMEM_SPEC, VMEM_SPEC, HBM_SPEC, VMEM_SPEC, HBM_SPEC],
        out_specs=[VMEM_SPEC] * 3,
        out_shape=[
            jax.ShapeDtypeStruct((512, DM), BF),
            jax.ShapeDtypeStruct((8, DM), F32),
            pltpu.VMEM((DM, HALF), BF),
        ],
        scratch_shapes=[pltpu.VMEM((8, 64, DM), F32), pltpu.SemaphoreType.DMA((9,))],
        compiler_params=pltpu.CompilerParams(vmem_limit_bytes=16 << 20),
        cost_estimate=pl.CostEstimate(flops=8_000_000, bytes_accessed=8_000_000, transcendentals=512),
        name="norm_backward",
    )(dest, cot, in_hbm(values.reshape(8, 64, DM)), gain, in_hbm(proj_t))


def token_kernel(pos_ref, grad_ref, left_ref, proj_t_hbm, own_hbm, other_hbm, *rest):
    out_ref, right_ref, sems = rest[0], rest[1], rest[6]
    right = pltpu.make_async_copy(proj_t_hbm.at[:, pl.ds(HALF, HALF)], right_ref, sems.at[0, 0])
    right.start()
    copies = [right]
    for i, hbm in enumerate((own_hbm, other_hbm)):
        x = (pos_ref[0] + 2) & 3
        y = (pos_ref[2] + 2) & 3
        rows = pl.ds(pl.multiple_of(x * XCONV, 64), XCONV)
        copies.append(pltpu.make_async_copy(hbm.at[rows], rest[2 + i], sems.at[0, 1 + i]))
        for k in range(NX):
            rows = pl.ds(pl.multiple_of(k * XCONV + y * YROWS, 16), YROWS)
            to = rest[4 + i].at[pl.ds(k * YROWS, YROWS)]
            copies.append(pltpu.make_async_copy(hbm.at[rows], to, sems.at[1 + i, k]))
    for copy in copies[1:]:
        copy.start()
    out_ref[:, :HALF] = dot(grad_ref[...], left_ref[...], ((1,), (0,))).astype(BF)
    right.wait()
    out_ref[:, HALF:] = dot(grad_ref[...], right_ref[...], ((1,), (0,))).astype(BF)
    for copy in copies[1:]:
        copy.wait()


def token_grad(pos, grads, left, proj_t, own, other):
    return pl.pallas_call(
        token_kernel,
        in_specs=[SMEM_SPEC, VMEM_SPEC, VMEM_SPEC, HBM_SPEC, HBM_SPEC, HBM_SPEC],
        out_specs=[VMEM_SPEC] * 6,
        out_shape=[jax.ShapeDtypeStruct((512, COUT), BF), pltpu.VMEM((DM, HALF), BF)]
        + [pltpu.VMEM((XCONV, 512), BF)] * 4,
        scratch_shapes=[pltpu.SemaphoreType.DMA((3, 4))],
        compiler_params=pltpu.CompilerParams(vmem_limit_bytes=16 << 20),
        cost_estimate=pl.CostEstimate(flops=1_340_000_000, bytes_accessed=8_000_000, transcendentals=0),
        name="token_grad",
    )(pos, grads, left, in_hbm(proj_t), in_hbm(own), in_hbm(other))


def by_turn(axis, pos_ref, s, rows_ref):
    if axis == 0:
        return rows_ref[(pos_ref[0] + s) & 3]
    rows = pl.ds(pl.multiple_of(((pos_ref[2] + s) & 3) * YROWS, 16), YROWS)
    return jnp.concatenate([rows_ref[x, rows, :] for x in range(NX)], axis=0)


def conv_first_kernel(gtok, gother, left, right, own_x, other_x, own_y, other_y, own_hbm, other_hbm, after, *rest):
    outs, gtok_other, brought, gtok_hbm, gtok_other_hbm = rest[:4], rest[4], rest[5:7], rest[7], rest[8]
    part, sems, in_sems, g_sems = rest[9:]
    moves = [
        pltpu.make_async_copy(hbm.at[pl.ds(NX * XCONV, NX * XPROJ)], brought[i], in_sems.at[i])
        for i, hbm in enumerate((own_hbm, other_hbm))
    ]
    moves.append(pltpu.make_async_copy(gtok, gtok_hbm, g_sems.at[0]))
    for copy in moves:
        copy.start()
    for slot, (weights, mine, theirs) in enumerate(((left, own_x, other_x), (right, own_y, other_y))):
        at = pl.ds(slot * HALF, HALF)
        gtok_other[:, at] = dot(gother[...], weights[...], ((1,), (0,))).astype(BF)
        moves.append(pltpu.make_async_copy(gtok_other.at[:, at], gtok_other_hbm.at[:, at], g_sems.at[1 + slot]))
        moves[-1].start()
        part[slot] = (
            dot(mine[...], gtok[:, at], ((1,), (0,))) + dot(theirs[...], gtok_other[:, at], ((1,), (0,)))
        ).astype(BF)
        for half in range(2):
            rows = part.at[slot, pl.ds(half * HROWS, HROWS)]
            moves.append(pltpu.make_async_copy(rows, outs[2 * slot + half], sems.at[slot, half]))
            moves[-1].start()
    for copy in moves:
        copy.wait()


def conv_first(gtok, gother, left, right, blocks, own, other, after):
    return pl.pallas_call(
        conv_first_kernel,
        in_specs=[VMEM_SPEC] * 8 + [HBM_SPEC] * 2 + [ANY_SPEC],
        out_specs=[HBM_SPEC] * 4 + [VMEM_SPEC] * 3 + [HBM_SPEC] * 2,
        out_shape=[pltpu.HBM((HROWS, HALF), BF)] * 4
        + [jax.ShapeDtypeStruct((512, COUT), BF)]
        + [pltpu.VMEM((NX * XPROJ, 512), BF)] * 2
        + [pltpu.HBM((512, COUT), BF)] * 2,
        scratch_shapes=[
            pltpu.VMEM((2, XCONV, HALF), BF),
            pltpu.SemaphoreType.DMA((2, 2)),
            pltpu.SemaphoreType.DMA((2,)),
            pltpu.SemaphoreType.DMA((3,)),
        ],
        compiler_params=pltpu.CompilerParams(vmem_limit_bytes=16 << 20),
        cost_estimate=pl.CostEstimate(flops=2_500_000_000, bytes_accessed=8_000_000, transcendentals=0),
        name="conv_first",
    )(gtok, gother, left, right, *blocks, in_hbm(own), in_hbm(other), after)


def conv_second_kernel(pos_ref, own_hbm, other_hbm, gtok_hbm, gtok_other_hbm, after, *rest):
    outs, own, other, gtok, gtok_other, part, sems, in_sems, g_sems = rest[:6], *rest[6:]
    grads = [
        pltpu.make_async_copy(gtok_hbm, gtok, g_sems.at[0]),
        pltpu.make_async_copy(gtok_other_hbm, gtok_other, g_sems.at[1]),
    ]
    blocks = []
    for s in (1, 3, 0, 2):
        x = (pos_ref[0] + s) & 3
        rows = pl.ds(pl.multiple_of(x * XCONV, 64), XCONV)
        blocks.append(
            [
                pltpu.make_async_copy(hbm.at[rows], vmem.at[x], in_sems.at[i, s])
                for i, (hbm, vmem) in enumerate(((own_hbm, own), (other_hbm, other)))
            ]
        )
    for copy in (blocks[0][0], grads[0], blocks[0][1], grads[1], *blocks[1]):
        copy.start()
    sends = []
    for axis in (0, 2):
        for s in (1, 3, 0):
            slot = len(sends)
            if slot == 0:
                for copy in grads:
                    copy.wait()
            if slot < 2:
                for copy in blocks[slot + 2]:
                    copy.start()
            for block in {0: blocks[:1], 1: blocks[1:2], 2: blocks[2:3], 3: blocks[3:]}.get(slot, []):
                for copy in block:
                    copy.wait()
            at = pl.ds(axis * HALF // 2, HALF)
            part[slot] = (
                dot(by_turn(axis, pos_ref, s, own), gtok[:, at], ((1,), (0,)))
                + dot(by_turn(axis, pos_ref, s, other), gtok_other[:, at], ((1,), (0,)))
            ).astype(BF)
            sends.append(pltpu.make_async_copy(part.at[slot], outs[slot], sems.at[slot]))
            sends[-1].start()
    for copy in sends:
        copy.wait()


def conv_second(pos, own, other, gtok, gtok_other, after):
    return pl.pallas_call(
        conv_second_kernel,
        in_specs=[SMEM_SPEC] + [HBM_SPEC] * 5,
        out_specs=[HBM_SPEC] * 6,
        out_shape=[pltpu.HBM((XCONV, HALF), BF)] * 6,
        scratch_shapes=[
            pltpu.VMEM((NX, XCONV, 512), BF),
            pltpu.VMEM((NX, XCONV, 512), BF),
            pltpu.VMEM((512, COUT), BF),
            pltpu.VMEM((512, COUT), BF),
            pltpu.VMEM((6, XCONV, HALF), BF),
            pltpu.SemaphoreType.DMA((6,)),
            pltpu.SemaphoreType.DMA((2, 4)),
            pltpu.SemaphoreType.DMA((2,)),
        ],
        compiler_params=pltpu.CompilerParams(vmem_limit_bytes=24 << 20),
        cost_estimate=pl.CostEstimate(flops=COST_SECOND, bytes_accessed=3_000_000, transcendentals=0),
        name="conv_second",
    )(pos, *[in_hbm(a) for a in (own, other, gtok, gtok_other, after)])


def add_kernel(ahead_in, behind_in, from_behind, from_ahead, ahead, behind, part, sems):
    halves = (
        (ahead_in, ahead, pl.ds(0, HROWS), from_behind),
        (behind_in, behind, pl.ds(HROWS, HROWS), from_ahead),
    )
    loads = [
        pltpu.make_async_copy(old.at[rows], part.at[i], sems.at[0, i]) for i, (old, _, rows, _) in enumerate(halves)
    ]
    stores = [
        pltpu.make_async_copy(part.at[i], new.at[rows], sems.at[1, i]) for i, (_, new, rows, _) in enumerate(halves)
    ]
    for copy in loads:
        copy.start()
    for i in range(2):
        loads[i].wait()
        part[i] = (part[i].astype(F32) + halves[i][3][...].astype(F32)).astype(BF)
        stores[i].start()
    for copy in stores:
        copy.wait()


def relay(axis, halves, ahead, behind, here):
    forward, back = [(i, (i + 1) % 4) for i in range(4)], [(i, (i + 3) % 4) for i in range(4)]
    from_behind = lax.ppermute(halves[0], axis, forward)
    from_ahead = lax.ppermute(halves[1], axis, back)

    def finish():
        one, other = pl.pallas_call(
            add_kernel,
            in_specs=[HBM_SPEC, HBM_SPEC, VMEM_SPEC, VMEM_SPEC],
            out_specs=[HBM_SPEC] * 2,
            out_shape=[pltpu.HBM((XCONV, HALF), BF)] * 2,
            input_output_aliases={0: 0, 1: 1},
            scratch_shapes=[pltpu.VMEM((2, HROWS, HALF), BF), pltpu.SemaphoreType.DMA((2, 2))],
            compiler_params=pltpu.CompilerParams(vmem_limit_bytes=16 << 20),
            cost_estimate=pl.CostEstimate(flops=COST_ADD, bytes_accessed=3_000_000, transcendentals=0),
            name="add_" + axis,
        )(in_hbm(ahead), in_hbm(behind), from_behind, from_ahead)
        return [here, lax.ppermute(one, axis, forward), lax.ppermute(other, axis, back)]

    return finish()


def split_gain(gain):
    high = gain.astype(BF).astype(F32)
    rest = gain - high
    low = rest.astype(BF).astype(F32)
    return jnp.concatenate(
        [
            jnp.broadcast_to(high, (8, DM)),
            jnp.broadcast_to(low, (8, DM)),
        ],
        axis=0,
    )


def proj_kernel(own, other, gown, gother, gain_own, gain_other, after, out_hbm, stage, out, sem):
    gain = split_gain(gain_own[0:1] + gain_other[0:1]).astype(BF)
    for x in range(4):
        rows = slice(x * XPROJ, (x + 1) * XPROJ)
        part = dot(own[rows, :], gown[...], ((1,), (0,))) + dot(other[rows, :], gother[...], ((1,), (0,)))
        for y in range(4):
            for z in range(4):
                stage[z, y * 32 + x * 8 : y * 32 + x * 8 + 8, :] = part[y * 32 + z * 8 : y * 32 + z * 8 + 8]
    for z in range(4):
        out[z, 0:128, :] = stage[z].astype(BF)
        out[z, 128:144, :] = gain
    copy = pltpu.make_async_copy(out, out_hbm, sem)
    copy.start()
    copy.wait()


def proj_grad(own, other, gown, gother, gain_own, gain_other, after):
    return pl.pallas_call(
        proj_kernel,
        in_specs=[VMEM_SPEC] * 6 + [ANY_SPEC],
        out_specs=HBM_SPEC,
        out_shape=pltpu.HBM((4, 144, DM), BF),
        scratch_shapes=[
            pltpu.VMEM((4, XPROJ, DM), F32),
            pltpu.VMEM((4, 144, DM), BF),
            pltpu.SemaphoreType.DMA,
        ],
        compiler_params=pltpu.CompilerParams(vmem_limit_bytes=16 << 20),
        cost_estimate=pl.CostEstimate(flops=COST_PROJ, bytes_accessed=2_000_000, transcendentals=0),
        name="proj_grad",
    )(own, other, gown, gother, gain_own, gain_other, after)


def small(kernel, name, outs, args, scratch=(), mib=16, flops=1_000_000, after=()):
    bytes_in = sum(a.size * a.dtype.itemsize for a in args)
    return pl.pallas_call(
        kernel,
        in_specs=[SMEM_SPEC] + [VMEM_SPEC] * (len(args) - 1) + [ANY_SPEC] * len(after),
        out_specs=[VMEM_SPEC] * len(outs),
        out_shape=[jax.ShapeDtypeStruct(*o) for o in outs],
        scratch_shapes=list(scratch),
        compiler_params=pltpu.CompilerParams(vmem_limit_bytes=mib << 20),
        cost_estimate=pl.CostEstimate(flops=flops, bytes_accessed=bytes_in, transcendentals=0),
        name=name,
    )(*args, *after)


def first_sum_kernel(pos_ref, a, b, c, *outs):
    for s, ref in enumerate(outs):
        at = pl.ds(pl.multiple_of(((pos_ref[2] + s) & 3) * YROWS, 16), YROWS)
        ref[...] = (a[at, :].astype(F32) + (b[at, :].astype(F32) + c[at, :].astype(F32))).astype(BF)


def sum_four(ref, rows, gain_rows):
    got = [ref[i, 0:rows, :].astype(F32) for i in range(4)]
    high, low = pl.ds(gain_rows, 8), pl.ds(gain_rows + 8, 8)
    gains = [ref[i, high, :].astype(F32) + ref[i, low, :].astype(F32) for i in range(4)]
    gain = split_gain(((gains[0] + gains[1]) + (gains[2] + gains[3]))[0:1])
    return (got[0] + got[1]) + (got[2] + got[3]), gain


def proj_sum_kernel(pos_ref, got_ref, out_ref, gains):
    total, gain = sum_four(got_ref, 128, 128)
    gains[...] = jnp.zeros_like(gains)
    for t in range(DM // 128):
        piece = slice(128 * t, 128 * t + 128)
        gains[t : t + 1, 0:128] = gain[0:1, piece]
        gains[t : t + 1, 128:256] = gain[8:9, piece]
    for k in range(16):
        rows = total[8 * k : 8 * k + 8]
        halves = jnp.concatenate([rows[:, : DM // 2], rows[:, DM // 2 :]], axis=0)
        out_ref[k] = jnp.concatenate([halves, gains[...]], axis=1).astype(BF)


def second_sum_kernel(pos_ref, a, b, c, o0, o1, o2, o3, part, by_z):
    part[...] = a[...].astype(F32) + (b[...].astype(F32) + c[...].astype(F32))
    for x in range(4):
        for z in range(4):
            at = x * YROWS + z * CONV_ROWS
            by_z[z, x * CONV_ROWS : (x + 1) * CONV_ROWS, :] = part[at : at + CONV_ROWS, :]
    for s, ref in enumerate((o0, o1, o2, o3)):
        ref[...] = by_z[(pos_ref[3] + s) & 3].astype(BF)


def plane_sum_kernel(along, pos_ref, a, b, c, d, o0, o1, o2, o3, part, split):
    part[...] = (a[...].astype(F32) + b[...].astype(F32)) + (c[...].astype(F32) + d[...].astype(F32))
    for i in range(4):
        split[i, 0:CONV_ROWS, :] = part[CONV_ROWS * i : CONV_ROWS * (i + 1), :]
    for s, ref in enumerate((o0, o1, o2, o3)):
        ref[...] = split[(pos_ref[along] + s) & 3, 0:CONV_ROWS, :].astype(BF)


def conv_total_kernel(pos_ref, a0, a1, a2, a3, b0, b1, b2, b3, after, out_ref):
    for at, refs in ((0, (a0, a1, a2, a3)), (HALF, (b0, b1, b2, b3))):
        p, q, r, t = [ref[...].astype(F32) for ref in refs]
        out_ref[:, at : at + HALF] = (p + q) + (r + t)


def proj_total_kernel(pos_ref, got_ref, out_ref, gain_ref):
    total = got_ref[0].astype(F32)
    for i in range(1, 16):
        total = total + got_ref[i].astype(F32)
    out_ref[:, : DM // 2] = total[0:8, : DM // 2]
    out_ref[:, DM // 2 :] = total[8:16, : DM // 2]
    gains = total[:, DM // 2 : DM // 2 + 128] + total[:, DM // 2 + 128 :]
    for t in range(DM // 128):
        gain_ref[:, 128 * t : 128 * t + 128] = gains[t : t + 1]


def turn(axis, parts):
    return [parts[0]] + [
        lax.ppermute(parts[s], axis, [(i, (i + s) % 4) for i in range(4)]) for s in (1, 2, 3)
    ]


def per_device(pre_conv, conv_weight, proj_weight, norm_gain, slab_cotangent, page_tiles, block_dest):
    pos = jnp.stack([lax.axis_index(axis) for axis in ALL]).astype(jnp.int32)
    swap = functools.partial(lax.ppermute, axis_name="core", perm=[(0, 1), (1, 0)])
    cot = lax.all_to_all(slab_cotangent.reshape(16, 64, DM), ("y", "z"), 0, 0, tiled=True)
    own, other, values, proj_t = forward(
        pos, page_tiles, pre_conv.reshape(2048, CIN), conv_weight, proj_weight
    )
    other = swap(other)
    grads, gain, left = norm(block_dest[:, 0], cot, values, norm_gain.reshape(1, DM), proj_t)
    gother, gain_other = swap(grads), swap(gain)

    gtok, right, *blocks = token_grad(pos, grads, left, proj_t, own, other)
    *halves, gtok_other, my_tokens, their_tokens, gtok, gtok_far = conv_first(
        gtok, gother, left, right, blocks, own, other, gain_other
    )
    proj = proj_grad(my_tokens, their_tokens, grads, gother, gain, gain_other, gtok_other)
    shares = conv_second(pos, own, other, gtok, gtok_far, proj)
    proj = lax.all_to_all(proj, "z", 0, 0, tiled=True)
    first = relay("x", halves[:2], *shares[:3])
    second = relay("y", halves[2:], *shares[3:])

    plane = ((YROWS, HALF), BF)
    (proj,) = small(proj_sum_kernel, "proj_sum", [((16, 16, DM // 2 + 256), BF)], [pos, proj], [pltpu.VMEM((16, 256), F32)])
    first = turn("y", small(first_sum_kernel, "first_sum", [plane] * 4, [pos, *first], flops=COST_SUM))
    second = small(
        second_sum_kernel,
        "second_sum",
        [plane] * 4,
        [pos, *second],
        [pltpu.VMEM((XCONV, HALF), F32), pltpu.VMEM((4, YROWS, HALF), F32)],
        flops=COST_SUM,
    )
    second = turn("z", second)
    proj = lax.all_to_all(proj, ("y", "x"), 0, 0, tiled=True)
    grad_proj, grad_gain = small(
        proj_total_kernel, "proj_total", [((PROJ_ROWS, DM), F32), ((1, DM), F32)], [pos, proj]
    )
    lines = ((CONV_ROWS, HALF), BF)
    scratch = [pltpu.VMEM((YROWS, HALF), F32), pltpu.VMEM((4, 40, HALF), F32)]
    second = small(
        functools.partial(plane_sum_kernel, 0), "plane_sum_x", [lines] * 4, [pos, *second], scratch, flops=COST_SUM
    )
    first = small(
        functools.partial(plane_sum_kernel, 3), "plane_sum_z", [lines] * 4, [pos, *first], scratch, flops=COST_SUM
    )
    (grad_conv,) = small(
        conv_total_kernel,
        "conv_total",
        [((CONV_ROWS, COUT), F32)],
        [pos, *turn("z", first), *turn("x", second)],
        flops=COST_SUM,
        after=[grad_gain],
    )
    return grad_conv, grad_proj, grad_gain.reshape(DM)


def solution(mesh):
    split = Mesh(mesh.devices.reshape(4, 2, 4, 4), ALL)
    return jax.shard_map(
        per_device,
        mesh=split,
        in_specs=(P(ALL), P(), P(), P(), P(ALL), P(ALL), P(ALL)),
        out_specs=(P(ALL), P(ALL), P()),
        check_vma=False,
    )
```

```python
import functools

import jax
import jax.numpy as jnp
from jax import lax
from jax.experimental import pallas as pl
from jax.experimental.pallas import tpu as pltpu
from jax.sharding import Mesh
from jax.sharding import PartitionSpec as P

EPS = 1e-6
BF = jnp.bfloat16
F32 = jnp.float32
ALL = ("x", "core", "y", "z")
CHIPS = ("x", "y", "z")

CIN = 512
COUT = 1024
DM = 1280
TOK = 256
SIDE = 16
NX = 4
NYZ = 16
CONV_ROWS = 36
PROJ_ROWS = 8
XCONV = CONV_ROWS * NYZ
XPROJ = PROJ_ROWS * NYZ
XROWS = XCONV + XPROJ
YROWS = XCONV // 4
HROWS = XCONV // 2
HALF = COUT // 2
COST_ADD = 1
COST_SUM = 1
COST_PROJ = 20000000000
COST_SECOND = 20000000000


def dot(a, b, dims):
    return lax.dot_general(a, b, (dims, ((), ())), preferred_element_type=F32)


def selection():
    row = lax.broadcasted_iota(jnp.int32, (384, 256), 0)
    col = lax.broadcasted_iota(jnp.int32, (384, 256), 1)
    tap = lax.shift_right_logical(row, 7)
    parity = lax.shift_right_logical(row, 6) & 1
    y = lax.shift_right_logical(row, 4) & 3
    x = 2 * (row & 15) + tap - 1
    hit = (col == (2 * y + parity) * 32 + x) & (x >= 0)
    return jnp.where(hit, 1.0, 0.0)


def forward_kernel(
    core_ref, pages_ref, pre_ref, w_ref, proj_ref, own_ref, other_ref, values_ref, proj_t_ref, patch, patch_t, acc
):
    step = pl.program_id(0)

    @pl.when(step == 0)
    def _():
        select = selection()
        for t in range(2):
            live = jnp.where(t < pages_ref[0], 1.0, 0.0)
            chosen = (select * live).astype(BF)
            for c in range(3):
                patch[t * TOK : t * TOK + SIDE, c * CIN : (c + 1) * CIN] = jnp.zeros((SIDE, CIN), BF)
            for q in range(4):
                rows = pre_ref[t * 1024 + q * 256 : t * 1024 + (q + 1) * 256, :]
                got = dot(chosen, rows, ((1,), (0,))).astype(BF)
                at = t * TOK + q * 64
                for c in range(3):
                    even = got[c * 128 : c * 128 + 64]
                    odd = got[c * 128 + 64 : c * 128 + 128]
                    patch[at : at + 64, (3 + c) * CIN : (4 + c) * CIN] = even
                    patch[at : at + 64, (6 + c) * CIN : (7 + c) * CIN] = odd
                    if q < 3:
                        patch[at + 16 : at + 80, c * CIN : (c + 1) * CIN] = odd
                    else:
                        patch[at + 16 : at + 64, c * CIN : (c + 1) * CIN] = odd[:48]

    for k in range(9):

        @pl.when(step == k)
        def _(k=k):
            taps = patch[:, k * CIN : (k + 1) * CIN]
            part = dot(taps, w_ref[...], ((1,), (0,)))
            if k == 0:
                acc[...] = part
            else:
                acc[...] += part
            patch_t[k * CIN : (k + 1) * CIN, :] = taps.T

    @pl.when(step == 8)
    def _():
        tokens = acc[...].astype(BF)
        values_ref[...] = dot(tokens, proj_ref[...], ((1,), (0,)))
        proj_t_ref[...] = proj_ref[...].T
        patch_t[9 * CIN : 9 * CIN + COUT, :] = tokens.T
        core = core_ref[1]
        for x in range(NX):
            for who, ref in ((core, own_ref), (1 - core, other_ref)):
                a = 2 * x + who
                conv_at = pl.multiple_of(a * XCONV, 64)
                proj_at = pl.multiple_of(9 * CIN + a * XPROJ, 128)
                ref[x * XCONV : (x + 1) * XCONV, :] = patch_t[pl.ds(conv_at, XCONV), :]
                to = NX * XCONV + x * XPROJ
                ref[to : to + XPROJ, :] = patch_t[pl.ds(proj_at, XPROJ), :]


def forward(core, pages, pre, w, proj):
    n = 2 * TOK
    smem = pl.BlockSpec(memory_space=pltpu.SMEM)
    return pl.pallas_call(
        forward_kernel,
        grid=(9,),
        in_specs=[
            smem,
            smem,
            pl.BlockSpec((2048, CIN), lambda k: (0, 0)),
            pl.BlockSpec((CIN, COUT), lambda k: (k, 0)),
            pl.BlockSpec((COUT, DM), lambda k: (0, 0)),
        ],
        out_specs=[
            pl.BlockSpec((NX * XROWS, n), lambda k: (0, 0)),
            pl.BlockSpec((NX * XROWS, n), lambda k: (0, 0)),
            pl.BlockSpec((n, DM), lambda k: (0, 0)),
            pl.BlockSpec((DM, COUT), lambda k: (0, 0)),
        ],
        out_shape=[
            jax.ShapeDtypeStruct((NX * XROWS, n), BF),
            jax.ShapeDtypeStruct((NX * XROWS, n), BF),
            jax.ShapeDtypeStruct((n, DM), F32),
            jax.ShapeDtypeStruct((DM, COUT), BF),
        ],
        scratch_shapes=[
            pltpu.VMEM((n, 9 * CIN), BF),
            pltpu.VMEM((9 * CIN + COUT, n), BF),
            pltpu.VMEM((n, COUT), F32),
        ],
        compiler_params=pltpu.CompilerParams(vmem_limit_bytes=60 << 20),
        cost_estimate=pl.CostEstimate(flops=6_200_000_000, bytes_accessed=24_000_000, transcendentals=0),
        name="forward",
    )(core, pages, pre, w, proj)


def norm_kernel(
    dest_ref, cot_ref, values_hbm, gain_ref, proj_t_hbm, grad_ref, gain_out_ref, proj_t_ref, values, sems
):
    copies = [pltpu.make_async_copy(values_hbm.at[k], values.at[k], sems.at[k]) for k in range(8)]
    copies.append(pltpu.make_async_copy(proj_t_hbm.at[:, pl.ds(0, HALF)], proj_t_ref, sems.at[8]))
    for copy in copies:
        copy.start()
    total = jnp.zeros((8, DM), F32)
    for k in range(8):
        c = cot_ref[dest_ref[k]].astype(F32)
        copies[k].wait()
        v = values[k]
        scale = lax.rsqrt(jnp.mean(v * v, axis=-1, keepdims=True) + EPS)
        up = c * gain_ref[...]
        inner = jnp.mean(up * v, axis=-1, keepdims=True)
        grad_ref[64 * k : 64 * k + 64, :] = (scale * up - v * (scale * scale * scale * inner)).astype(BF)
        total = total + jnp.sum((c * v * scale).reshape(8, 8, DM), axis=0)
    gain_out_ref[...] = jnp.broadcast_to(jnp.sum(total, axis=0, keepdims=True), (8, DM))
    copies[8].wait()


SMEM_SPEC = pl.BlockSpec(memory_space=pltpu.SMEM)
VMEM_SPEC = pl.BlockSpec(memory_space=pltpu.VMEM)
HBM_SPEC = pl.BlockSpec(memory_space=pltpu.HBM)
ANY_SPEC = pl.BlockSpec(memory_space=pl.ANY)


def in_hbm(array):
    return pltpu.with_memory_space_constraint(array, pltpu.HBM)


def norm(dest, cot, values, gain, proj_t):
    return pl.pallas_call(
        norm_kernel,
        in_specs=[SMEM_SPEC, VMEM_SPEC, HBM_SPEC, VMEM_SPEC, HBM_SPEC],
        out_specs=[VMEM_SPEC] * 3,
        out_shape=[
            jax.ShapeDtypeStruct((512, DM), BF),
            jax.ShapeDtypeStruct((8, DM), F32),
            pltpu.VMEM((DM, HALF), BF),
        ],
        scratch_shapes=[pltpu.VMEM((8, 64, DM), F32), pltpu.SemaphoreType.DMA((9,))],
        compiler_params=pltpu.CompilerParams(vmem_limit_bytes=16 << 20),
        cost_estimate=pl.CostEstimate(flops=8_000_000, bytes_accessed=8_000_000, transcendentals=512),
        name="norm_backward",
    )(dest, cot, in_hbm(values.reshape(8, 64, DM)), gain, in_hbm(proj_t))


def token_kernel(pos_ref, grad_ref, left_ref, proj_t_hbm, own_hbm, other_hbm, *rest):
    out_ref, right_ref, sems = rest[0], rest[1], rest[8]
    right = pltpu.make_async_copy(proj_t_hbm.at[:, pl.ds(HALF, HALF)], right_ref, sems.at[0, 0])
    right.start()
    copies = [right]
    for i, hbm in enumerate((own_hbm, other_hbm)):
        x = (pos_ref[0] + 2) & 3
        y = (pos_ref[2] + 2) & 3
        rows = pl.ds(pl.multiple_of(x * XCONV, 64), XCONV)
        copies.append(pltpu.make_async_copy(hbm.at[rows], rest[2 + i], sems.at[0, 1 + i]))
        for k in range(NX):
            rows = pl.ds(pl.multiple_of(k * XCONV + y * YROWS, 16), YROWS)
            to = rest[4 + i].at[pl.ds(k * YROWS, YROWS)]
            copies.append(pltpu.make_async_copy(hbm.at[rows], to, sems.at[1 + i, k]))
        rows = pl.ds(NX * XCONV, NX * XPROJ)
        copies.append(pltpu.make_async_copy(hbm.at[rows], rest[6 + i], sems.at[3, i]))
    for copy in copies[1:]:
        copy.start()
    out_ref[:, :HALF] = dot(grad_ref[...], left_ref[...], ((1,), (0,))).astype(BF)
    right.wait()
    out_ref[:, HALF:] = dot(grad_ref[...], right_ref[...], ((1,), (0,))).astype(BF)
    for copy in copies[1:]:
        copy.wait()


def token_grad(pos, grads, left, proj_t, own, other):
    return pl.pallas_call(
        token_kernel,
        in_specs=[SMEM_SPEC, VMEM_SPEC, VMEM_SPEC, HBM_SPEC, HBM_SPEC, HBM_SPEC],
        out_specs=[VMEM_SPEC] * 8,
        out_shape=[jax.ShapeDtypeStruct((512, COUT), BF), pltpu.VMEM((DM, HALF), BF)]
        + [pltpu.VMEM((XCONV, 512), BF)] * 4
        + [pltpu.VMEM((NX * XPROJ, 512), BF)] * 2,
        scratch_shapes=[pltpu.SemaphoreType.DMA((4, 4))],
        compiler_params=pltpu.CompilerParams(vmem_limit_bytes=16 << 20),
        cost_estimate=pl.CostEstimate(flops=1_340_000_000, bytes_accessed=8_000_000, transcendentals=0),
        name="token_grad",
    )(pos, grads, left, in_hbm(proj_t), in_hbm(own), in_hbm(other))


def by_turn(axis, pos_ref, s, rows_ref):
    if axis == 0:
        return rows_ref[(pos_ref[0] + s) & 3]
    rows = pl.ds(pl.multiple_of(((pos_ref[2] + s) & 3) * YROWS, 16), YROWS)
    return jnp.concatenate([rows_ref[x, rows, :] for x in range(NX)], axis=0)


def conv_first_kernel(
    gtok, gother, left, right, own_x, other_x, own_y, other_y, own_tok, other_tok, gown, gain_own, gain_other, *rest
):
    outs, gtok_hbm, gtok_other_hbm, proj_hbm = rest[:4], *rest[4:7]
    gtok_other, part, stage, out, sems, g_sems = rest[7:]
    moves = [pltpu.make_async_copy(gtok, gtok_hbm, g_sems.at[0])]
    moves[0].start()
    for slot, (weights, mine, theirs) in enumerate(((left, own_x, other_x), (right, own_y, other_y))):
        at = pl.ds(slot * HALF, HALF)
        gtok_other[:, at] = dot(gother[...], weights[...], ((1,), (0,))).astype(BF)
        moves.append(pltpu.make_async_copy(gtok_other.at[:, at], gtok_other_hbm.at[:, at], g_sems.at[1 + slot]))
        moves[-1].start()
        part[slot] = (
            dot(mine[...], gtok[:, at], ((1,), (0,))) + dot(theirs[...], gtok_other[:, at], ((1,), (0,)))
        ).astype(BF)
        for half in range(2):
            rows = part.at[slot, pl.ds(half * HROWS, HROWS)]
            moves.append(pltpu.make_async_copy(rows, outs[2 * slot + half], sems.at[slot, half]))
            moves[-1].start()
    gain = split_gain(gain_own[0:1] + gain_other[0:1]).astype(BF)
    for x in range(4):
        rows = slice(x * XPROJ, (x + 1) * XPROJ)
        share = dot(own_tok[rows, :], gown[...], ((1,), (0,))) + dot(other_tok[rows, :], gother[...], ((1,), (0,)))
        for y in range(4):
            for z in range(4):
                stage[z, y * 32 + x * 8 : y * 32 + x * 8 + 8, :] = share[y * 32 + z * 8 : y * 32 + z * 8 + 8]
    for z in range(4):
        out[z, 0:128, :] = stage[z].astype(BF)
        out[z, 128:144, :] = gain
        moves.append(pltpu.make_async_copy(out.at[z], proj_hbm.at[z], g_sems.at[3 + z]))
        moves[-1].start()
    for copy in moves:
        copy.wait()


def conv_first(gtok, gother, left, right, blocks, grads, gain, gain_other):
    return pl.pallas_call(
        conv_first_kernel,
        in_specs=[VMEM_SPEC] * 13,
        out_specs=[HBM_SPEC] * 7,
        out_shape=[pltpu.HBM((HROWS, HALF), BF)] * 4
        + [pltpu.HBM((512, COUT), BF)] * 2
        + [pltpu.HBM((4, 144, DM), BF)],
        scratch_shapes=[
            pltpu.VMEM((512, COUT), BF),
            pltpu.VMEM((2, XCONV, HALF), BF),
            pltpu.VMEM((4, XPROJ, DM), F32),
            pltpu.VMEM((4, 144, DM), BF),
            pltpu.SemaphoreType.DMA((2, 2)),
            pltpu.SemaphoreType.DMA((7,)),
        ],
        compiler_params=pltpu.CompilerParams(vmem_limit_bytes=24 << 20),
        cost_estimate=pl.CostEstimate(flops=4_000_000_000, bytes_accessed=8_000_000, transcendentals=0),
        name="conv_first",
    )(gtok, gother, left, right, *blocks, grads, gain, gain_other)


def conv_second_kernel(pos_ref, own_hbm, other_hbm, gtok_hbm, gtok_other_hbm, after, *rest):
    outs, own, other, gtok, gtok_other, part, sems, in_sems, g_sems = rest[:6], *rest[6:]
    grads = [
        pltpu.make_async_copy(gtok_hbm, gtok, g_sems.at[0]),
        pltpu.make_async_copy(gtok_other_hbm, gtok_other, g_sems.at[1]),
    ]
    blocks = []
    for s in (1, 3, 0, 2):
        x = (pos_ref[0] + s) & 3
        rows = pl.ds(pl.multiple_of(x * XCONV, 64), XCONV)
        blocks.append(
            [
                pltpu.make_async_copy(hbm.at[rows], vmem.at[x], in_sems.at[i, s])
                for i, (hbm, vmem) in enumerate(((own_hbm, own), (other_hbm, other)))
            ]
        )
    for copy in (grads[0], blocks[0][0], grads[1], blocks[0][1], *blocks[1], *blocks[2], *blocks[3]):
        copy.start()
    sends = []
    for axis in (0, 2):
        for s in (1, 3, 0):
            slot = len(sends)
            if slot == 0:
                for copy in grads:
                    copy.wait()
            for block in {0: blocks[:1], 1: blocks[1:2], 2: blocks[2:3], 3: blocks[3:]}.get(slot, []):
                for copy in block:
                    copy.wait()
            at = pl.ds(axis * HALF // 2, HALF)
            part[slot] = (
                dot(by_turn(axis, pos_ref, s, own), gtok[:, at], ((1,), (0,)))
                + dot(by_turn(axis, pos_ref, s, other), gtok_other[:, at], ((1,), (0,)))
            ).astype(BF)
            sends.append(pltpu.make_async_copy(part.at[slot], outs[slot], sems.at[slot]))
            sends[-1].start()
    for copy in sends:
        copy.wait()


def conv_second(pos, own, other, gtok, gtok_other, after):
    return pl.pallas_call(
        conv_second_kernel,
        in_specs=[SMEM_SPEC] + [HBM_SPEC] * 5,
        out_specs=[HBM_SPEC] * 6,
        out_shape=[pltpu.HBM((XCONV, HALF), BF)] * 6,
        scratch_shapes=[
            pltpu.VMEM((NX, XCONV, 512), BF),
            pltpu.VMEM((NX, XCONV, 512), BF),
            pltpu.VMEM((512, COUT), BF),
            pltpu.VMEM((512, COUT), BF),
            pltpu.VMEM((6, XCONV, HALF), BF),
            pltpu.SemaphoreType.DMA((6,)),
            pltpu.SemaphoreType.DMA((2, 4)),
            pltpu.SemaphoreType.DMA((2,)),
        ],
        compiler_params=pltpu.CompilerParams(vmem_limit_bytes=24 << 20),
        cost_estimate=pl.CostEstimate(flops=COST_SECOND, bytes_accessed=3_000_000, transcendentals=0),
        name="conv_second",
    )(pos, *[in_hbm(a) for a in (own, other, gtok, gtok_other, after)])


def add_kernel(ahead_in, behind_in, from_behind, from_ahead, ahead, behind, part, sems):
    halves = (
        (ahead_in, ahead, pl.ds(0, HROWS), from_behind),
        (behind_in, behind, pl.ds(HROWS, HROWS), from_ahead),
    )
    loads = [
        pltpu.make_async_copy(old.at[rows], part.at[i], sems.at[0, i]) for i, (old, _, rows, _) in enumerate(halves)
    ]
    stores = [
        pltpu.make_async_copy(part.at[i], new.at[rows], sems.at[1, i]) for i, (_, new, rows, _) in enumerate(halves)
    ]
    for copy in loads:
        copy.start()
    for i in range(2):
        loads[i].wait()
        part[i] = (part[i].astype(F32) + halves[i][3][...].astype(F32)).astype(BF)
        stores[i].start()
    for copy in stores:
        copy.wait()


def relay(axis, halves, ahead, behind, here):
    forward, back = [(i, (i + 1) % 4) for i in range(4)], [(i, (i + 3) % 4) for i in range(4)]
    from_behind = lax.ppermute(halves[0], axis, forward)
    from_ahead = lax.ppermute(halves[1], axis, back)

    def finish():
        one, other = pl.pallas_call(
            add_kernel,
            in_specs=[HBM_SPEC, HBM_SPEC, VMEM_SPEC, VMEM_SPEC],
            out_specs=[HBM_SPEC] * 2,
            out_shape=[pltpu.HBM((XCONV, HALF), BF)] * 2,
            input_output_aliases={0: 0, 1: 1},
            scratch_shapes=[pltpu.VMEM((2, HROWS, HALF), BF), pltpu.SemaphoreType.DMA((2, 2))],
            compiler_params=pltpu.CompilerParams(vmem_limit_bytes=16 << 20),
            cost_estimate=pl.CostEstimate(flops=COST_ADD, bytes_accessed=3_000_000, transcendentals=0),
            name="add_" + axis,
        )(in_hbm(ahead), in_hbm(behind), from_behind, from_ahead)
        return [here, lax.ppermute(one, axis, forward), lax.ppermute(other, axis, back)]

    return finish()


def split_gain(gain):
    high = gain.astype(BF).astype(F32)
    rest = gain - high
    low = rest.astype(BF).astype(F32)
    return jnp.concatenate(
        [
            jnp.broadcast_to(high, (8, DM)),
            jnp.broadcast_to(low, (8, DM)),
        ],
        axis=0,
    )


def small(kernel, name, outs, args, scratch=(), mib=16, flops=1_000_000, after=()):
    bytes_in = sum(a.size * a.dtype.itemsize for a in args)
    return pl.pallas_call(
        kernel,
        in_specs=[SMEM_SPEC] + [VMEM_SPEC] * (len(args) - 1) + [ANY_SPEC] * len(after),
        out_specs=[VMEM_SPEC] * len(outs),
        out_shape=[jax.ShapeDtypeStruct(*o) for o in outs],
        scratch_shapes=list(scratch),
        compiler_params=pltpu.CompilerParams(vmem_limit_bytes=mib << 20),
        cost_estimate=pl.CostEstimate(flops=flops, bytes_accessed=bytes_in, transcendentals=0),
        name=name,
    )(*args, *after)


def first_sum_kernel(pos_ref, a, b, c, *outs):
    for s, ref in enumerate(outs):
        at = pl.ds(pl.multiple_of(((pos_ref[2] + s) & 3) * YROWS, 16), YROWS)
        ref[...] = (a[at, :].astype(F32) + (b[at, :].astype(F32) + c[at, :].astype(F32))).astype(BF)


def sum_four(ref, rows, gain_rows):
    got = [ref[i, 0:rows, :].astype(F32) for i in range(4)]
    high, low = pl.ds(gain_rows, 8), pl.ds(gain_rows + 8, 8)
    gains = [ref[i, high, :].astype(F32) + ref[i, low, :].astype(F32) for i in range(4)]
    gain = split_gain(((gains[0] + gains[1]) + (gains[2] + gains[3]))[0:1])
    return (got[0] + got[1]) + (got[2] + got[3]), gain


def proj_sum_kernel(pos_ref, got_ref, out_ref, gains):
    total, gain = sum_four(got_ref, 128, 128)
    gains[...] = jnp.zeros_like(gains)
    for t in range(DM // 128):
        piece = slice(128 * t, 128 * t + 128)
        gains[t : t + 1, 0:128] = gain[0:1, piece]
        gains[t : t + 1, 128:256] = gain[8:9, piece]
    for k in range(16):
        rows = total[8 * k : 8 * k + 8]
        halves = jnp.concatenate([rows[:, : DM // 2], rows[:, DM // 2 :]], axis=0)
        out_ref[k] = jnp.concatenate([halves, gains[...]], axis=1).astype(BF)


def second_sum_kernel(pos_ref, a, b, c, o0, o1, o2, o3, part, by_z):
    part[...] = a[...].astype(F32) + (b[...].astype(F32) + c[...].astype(F32))
    for x in range(4):
        for z in range(4):
            at = x * YROWS + z * CONV_ROWS
            by_z[z, x * CONV_ROWS : (x + 1) * CONV_ROWS, :] = part[at : at + CONV_ROWS, :]
    for s, ref in enumerate((o0, o1, o2, o3)):
        ref[...] = by_z[(pos_ref[3] + s) & 3].astype(BF)


def plane_sum_kernel(along, pos_ref, a, b, c, d, o0, o1, o2, o3, part, split):
    part[...] = (a[...].astype(F32) + b[...].astype(F32)) + (c[...].astype(F32) + d[...].astype(F32))
    for i in range(4):
        split[i, 0:CONV_ROWS, :] = part[CONV_ROWS * i : CONV_ROWS * (i + 1), :]
    for s, ref in enumerate((o0, o1, o2, o3)):
        ref[...] = split[(pos_ref[along] + s) & 3, 0:CONV_ROWS, :].astype(BF)


def conv_total_kernel(pos_ref, a0, a1, a2, a3, b0, b1, b2, b3, after, out_ref):
    for at, refs in ((0, (a0, a1, a2, a3)), (HALF, (b0, b1, b2, b3))):
        p, q, r, t = [ref[...].astype(F32) for ref in refs]
        out_ref[:, at : at + HALF] = (p + q) + (r + t)


def proj_total_kernel(pos_ref, got_ref, out_ref, gain_ref):
    total = got_ref[0].astype(F32)
    for i in range(1, 16):
        total = total + got_ref[i].astype(F32)
    out_ref[:, : DM // 2] = total[0:8, : DM // 2]
    out_ref[:, DM // 2 :] = total[8:16, : DM // 2]
    gains = total[:, DM // 2 : DM // 2 + 128] + total[:, DM // 2 + 128 :]
    for t in range(DM // 128):
        gain_ref[:, 128 * t : 128 * t + 128] = gains[t : t + 1]


def turn(axis, parts):
    return [parts[0]] + [
        lax.ppermute(parts[s], axis, [(i, (i + s) % 4) for i in range(4)]) for s in (1, 2, 3)
    ]


def per_device(pre_conv, conv_weight, proj_weight, norm_gain, slab_cotangent, page_tiles, block_dest):
    pos = jnp.stack([lax.axis_index(axis) for axis in ALL]).astype(jnp.int32)
    swap = functools.partial(lax.ppermute, axis_name="core", perm=[(0, 1), (1, 0)])
    cot = lax.all_to_all(slab_cotangent.reshape(16, 64, DM), ("y", "z"), 0, 0, tiled=True)
    own, other, values, proj_t = forward(
        pos, page_tiles, pre_conv.reshape(2048, CIN), conv_weight, proj_weight
    )
    other = swap(other)
    grads, gain, left = norm(block_dest[:, 0], cot, values, norm_gain.reshape(1, DM), proj_t)
    gother, gain_other = swap(grads), swap(gain)

    gtok, right, *blocks = token_grad(pos, grads, left, proj_t, own, other)
    *halves, gtok, gtok_far, proj = conv_first(gtok, gother, left, right, blocks, grads, gain, gain_other)
    shares = conv_second(pos, own, other, gtok, gtok_far, proj)
    proj = lax.all_to_all(proj, "z", 0, 0, tiled=True)
    first = relay("x", halves[:2], *shares[:3])
    second = relay("y", halves[2:], *shares[3:])

    plane = ((YROWS, HALF), BF)
    (proj,) = small(proj_sum_kernel, "proj_sum", [((16, 16, DM // 2 + 256), BF)], [pos, proj], [pltpu.VMEM((16, 256), F32)])
    first = turn("y", small(first_sum_kernel, "first_sum", [plane] * 4, [pos, *first], flops=COST_SUM))
    second = small(
        second_sum_kernel,
        "second_sum",
        [plane] * 4,
        [pos, *second],
        [pltpu.VMEM((XCONV, HALF), F32), pltpu.VMEM((4, YROWS, HALF), F32)],
        flops=COST_SUM,
    )
    second = turn("z", second)
    proj = lax.all_to_all(proj, ("y", "x"), 0, 0, tiled=True)
    grad_proj, grad_gain = small(
        proj_total_kernel, "proj_total", [((PROJ_ROWS, DM), F32), ((1, DM), F32)], [pos, proj]
    )
    lines = ((CONV_ROWS, HALF), BF)
    scratch = [pltpu.VMEM((YROWS, HALF), F32), pltpu.VMEM((4, 40, HALF), F32)]
    second = small(
        functools.partial(plane_sum_kernel, 0), "plane_sum_x", [lines] * 4, [pos, *second], scratch, flops=COST_SUM
    )
    first = small(
        functools.partial(plane_sum_kernel, 3), "plane_sum_z", [lines] * 4, [pos, *first], scratch, flops=COST_SUM
    )
    (grad_conv,) = small(
        conv_total_kernel,
        "conv_total",
        [((CONV_ROWS, COUT), F32)],
        [pos, *turn("z", first), *turn("x", second)],
        flops=COST_SUM,
        after=[grad_gain],
    )
    return grad_conv, grad_proj, grad_gain.reshape(DM)


def solution(mesh):
    split = Mesh(mesh.devices.reshape(4, 2, 4, 4), ALL)
    return jax.shard_map(
        per_device,
        mesh=split,
        in_specs=(P(ALL), P(), P(), P(), P(ALL), P(ALL), P(ALL)),
        out_specs=(P(ALL), P(ALL), P()),
        check_vma=False,
    )
```

```python
import functools

import jax
import jax.numpy as jnp
from jax import lax
from jax.experimental import pallas as pl
from jax.experimental.pallas import tpu as pltpu
from jax.sharding import Mesh
from jax.sharding import PartitionSpec as P

EPS = 1e-6
BF = jnp.bfloat16
F32 = jnp.float32
ALL = ("x", "core", "y", "z")
CHIPS = ("x", "y", "z")

CIN = 512
COUT = 1024
DM = 1280
TOK = 256
SIDE = 16
NX = 4
NYZ = 16
CONV_ROWS = 36
PROJ_ROWS = 8
XCONV = CONV_ROWS * NYZ
XPROJ = PROJ_ROWS * NYZ
XROWS = XCONV + XPROJ
YROWS = XCONV // 4
HROWS = XCONV // 2
HALF = COUT // 2
COST_ADD = 1
COST_SUM = 1000000000
COST_PROJ = 20000000000
COST_SECOND = 20000000000


def dot(a, b, dims):
    return lax.dot_general(a, b, (dims, ((), ())), preferred_element_type=F32)


def selection():
    row = lax.broadcasted_iota(jnp.int32, (384, 256), 0)
    col = lax.broadcasted_iota(jnp.int32, (384, 256), 1)
    tap = lax.shift_right_logical(row, 7)
    parity = lax.shift_right_logical(row, 6) & 1
    y = lax.shift_right_logical(row, 4) & 3
    x = 2 * (row & 15) + tap - 1
    hit = (col == (2 * y + parity) * 32 + x) & (x >= 0)
    return jnp.where(hit, 1.0, 0.0)


def forward_kernel(
    core_ref, pages_ref, pre_ref, w_ref, proj_ref, own_ref, other_ref, values_ref, proj_t_ref, patch, patch_t, acc
):
    step = pl.program_id(0)

    @pl.when(step == 0)
    def _():
        select = selection()
        for t in range(2):
            live = jnp.where(t < pages_ref[0], 1.0, 0.0)
            chosen = (select * live).astype(BF)
            for c in range(3):
                patch[t * TOK : t * TOK + SIDE, c * CIN : (c + 1) * CIN] = jnp.zeros((SIDE, CIN), BF)
            for q in range(4):
                rows = pre_ref[t * 1024 + q * 256 : t * 1024 + (q + 1) * 256, :]
                got = dot(chosen, rows, ((1,), (0,))).astype(BF)
                at = t * TOK + q * 64
                for c in range(3):
                    even = got[c * 128 : c * 128 + 64]
                    odd = got[c * 128 + 64 : c * 128 + 128]
                    patch[at : at + 64, (3 + c) * CIN : (4 + c) * CIN] = even
                    patch[at : at + 64, (6 + c) * CIN : (7 + c) * CIN] = odd
                    if q < 3:
                        patch[at + 16 : at + 80, c * CIN : (c + 1) * CIN] = odd
                    else:
                        patch[at + 16 : at + 64, c * CIN : (c + 1) * CIN] = odd[:48]

    for k in range(9):

        @pl.when(step == k)
        def _(k=k):
            taps = patch[:, k * CIN : (k + 1) * CIN]
            part = dot(taps, w_ref[...], ((1,), (0,)))
            if k == 0:
                acc[...] = part
            else:
                acc[...] += part
            patch_t[k * CIN : (k + 1) * CIN, :] = taps.T

    @pl.when(step == 8)
    def _():
        tokens = acc[...].astype(BF)
        values_ref[...] = dot(tokens, proj_ref[...], ((1,), (0,)))
        proj_t_ref[...] = proj_ref[...].T
        patch_t[9 * CIN : 9 * CIN + COUT, :] = tokens.T
        core = core_ref[1]
        for x in range(NX):
            for who, ref in ((core, own_ref), (1 - core, other_ref)):
                a = 2 * x + who
                conv_at = pl.multiple_of(a * XCONV, 64)
                proj_at = pl.multiple_of(9 * CIN + a * XPROJ, 128)
                ref[x * XCONV : (x + 1) * XCONV, :] = patch_t[pl.ds(conv_at, XCONV), :]
                to = NX * XCONV + x * XPROJ
                ref[to : to + XPROJ, :] = patch_t[pl.ds(proj_at, XPROJ), :]


def forward(core, pages, pre, w, proj):
    n = 2 * TOK
    smem = pl.BlockSpec(memory_space=pltpu.SMEM)
    return pl.pallas_call(
        forward_kernel,
        grid=(9,),
        in_specs=[
            smem,
            smem,
            pl.BlockSpec((2048, CIN), lambda k: (0, 0)),
            pl.BlockSpec((CIN, COUT), lambda k: (k, 0)),
            pl.BlockSpec((COUT, DM), lambda k: (0, 0)),
        ],
        out_specs=[
            pl.BlockSpec((NX * XROWS, n), lambda k: (0, 0)),
            pl.BlockSpec((NX * XROWS, n), lambda k: (0, 0)),
            pl.BlockSpec((n, DM), lambda k: (0, 0)),
            pl.BlockSpec((DM, COUT), lambda k: (0, 0)),
        ],
        out_shape=[
            jax.ShapeDtypeStruct((NX * XROWS, n), BF),
            jax.ShapeDtypeStruct((NX * XROWS, n), BF),
            jax.ShapeDtypeStruct((n, DM), F32),
            jax.ShapeDtypeStruct((DM, COUT), BF),
        ],
        scratch_shapes=[
            pltpu.VMEM((n, 9 * CIN), BF),
            pltpu.VMEM((9 * CIN + COUT, n), BF),
            pltpu.VMEM((n, COUT), F32),
        ],
        compiler_params=pltpu.CompilerParams(vmem_limit_bytes=60 << 20),
        cost_estimate=pl.CostEstimate(flops=6_200_000_000, bytes_accessed=24_000_000, transcendentals=0),
        name="forward",
    )(core, pages, pre, w, proj)


def norm_kernel(
    dest_ref, cot_ref, values_hbm, gain_ref, proj_t_hbm, grad_ref, gain_out_ref, proj_t_ref, values, sems
):
    copies = [pltpu.make_async_copy(values_hbm.at[k], values.at[k], sems.at[k]) for k in range(8)]
    copies.append(pltpu.make_async_copy(proj_t_hbm.at[:, pl.ds(0, HALF)], proj_t_ref, sems.at[8]))
    for copy in copies:
        copy.start()
    total = jnp.zeros((8, DM), F32)
    for k in range(8):
        c = cot_ref[dest_ref[k]].astype(F32)
        copies[k].wait()
        v = values[k]
        scale = lax.rsqrt(jnp.mean(v * v, axis=-1, keepdims=True) + EPS)
        up = c * gain_ref[...]
        inner = jnp.mean(up * v, axis=-1, keepdims=True)
        grad_ref[64 * k : 64 * k + 64, :] = (scale * up - v * (scale * scale * scale * inner)).astype(BF)
        total = total + jnp.sum((c * v * scale).reshape(8, 8, DM), axis=0)
    gain_out_ref[...] = jnp.broadcast_to(jnp.sum(total, axis=0, keepdims=True), (8, DM))
    copies[8].wait()


SMEM_SPEC = pl.BlockSpec(memory_space=pltpu.SMEM)
VMEM_SPEC = pl.BlockSpec(memory_space=pltpu.VMEM)
HBM_SPEC = pl.BlockSpec(memory_space=pltpu.HBM)
ANY_SPEC = pl.BlockSpec(memory_space=pl.ANY)


def in_hbm(array):
    return pltpu.with_memory_space_constraint(array, pltpu.HBM)


def norm(dest, cot, values, gain, proj_t):
    return pl.pallas_call(
        norm_kernel,
        in_specs=[SMEM_SPEC, VMEM_SPEC, HBM_SPEC, VMEM_SPEC, HBM_SPEC],
        out_specs=[VMEM_SPEC] * 3,
        out_shape=[
            jax.ShapeDtypeStruct((512, DM), BF),
            jax.ShapeDtypeStruct((8, DM), F32),
            pltpu.VMEM((DM, HALF), BF),
        ],
        scratch_shapes=[pltpu.VMEM((8, 64, DM), F32), pltpu.SemaphoreType.DMA((9,))],
        compiler_params=pltpu.CompilerParams(vmem_limit_bytes=16 << 20),
        cost_estimate=pl.CostEstimate(flops=8_000_000, bytes_accessed=8_000_000, transcendentals=512),
        name="norm_backward",
    )(dest, cot, in_hbm(values.reshape(8, 64, DM)), gain, in_hbm(proj_t))


def token_kernel(pos_ref, grad_ref, left_ref, proj_t_hbm, own_hbm, other_hbm, *rest):
    out_ref, right_ref, sems = rest[0], rest[1], rest[8]
    right = pltpu.make_async_copy(proj_t_hbm.at[:, pl.ds(HALF, HALF)], right_ref, sems.at[0, 0])
    right.start()
    copies = [right]
    for i, hbm in enumerate((own_hbm, other_hbm)):
        x = (pos_ref[0] + 2) & 3
        y = (pos_ref[2] + 2) & 3
        rows = pl.ds(pl.multiple_of(x * XCONV, 64), XCONV)
        copies.append(pltpu.make_async_copy(hbm.at[rows], rest[2 + i], sems.at[0, 1 + i]))
        for k in range(NX):
            rows = pl.ds(pl.multiple_of(k * XCONV + y * YROWS, 16), YROWS)
            to = rest[4 + i].at[pl.ds(k * YROWS, YROWS)]
            copies.append(pltpu.make_async_copy(hbm.at[rows], to, sems.at[1 + i, k]))
        rows = pl.ds(NX * XCONV, NX * XPROJ)
        copies.append(pltpu.make_async_copy(hbm.at[rows], rest[6 + i], sems.at[3, i]))
    for copy in copies[1:]:
        copy.start()
    out_ref[:, :HALF] = dot(grad_ref[...], left_ref[...], ((1,), (0,))).astype(BF)
    right.wait()
    out_ref[:, HALF:] = dot(grad_ref[...], right_ref[...], ((1,), (0,))).astype(BF)
    for copy in copies[1:]:
        copy.wait()


def token_grad(pos, grads, left, proj_t, own, other):
    return pl.pallas_call(
        token_kernel,
        in_specs=[SMEM_SPEC, VMEM_SPEC, VMEM_SPEC, HBM_SPEC, HBM_SPEC, HBM_SPEC],
        out_specs=[VMEM_SPEC] * 8,
        out_shape=[jax.ShapeDtypeStruct((512, COUT), BF), pltpu.VMEM((DM, HALF), BF)]
        + [pltpu.VMEM((XCONV, 512), BF)] * 4
        + [pltpu.VMEM((NX * XPROJ, 512), BF)] * 2,
        scratch_shapes=[pltpu.SemaphoreType.DMA((4, 4))],
        compiler_params=pltpu.CompilerParams(vmem_limit_bytes=16 << 20),
        cost_estimate=pl.CostEstimate(flops=1_340_000_000, bytes_accessed=8_000_000, transcendentals=0),
        name="token_grad",
    )(pos, grads, left, in_hbm(proj_t), in_hbm(own), in_hbm(other))


def by_turn(axis, pos_ref, s, rows_ref):
    if axis == 0:
        return rows_ref[(pos_ref[0] + s) & 3]
    rows = pl.ds(pl.multiple_of(((pos_ref[2] + s) & 3) * YROWS, 16), YROWS)
    return jnp.concatenate([rows_ref[x, rows, :] for x in range(NX)], axis=0)


def conv_first_kernel(
    gtok, gother, left, right, own_x, other_x, own_y, other_y, own_tok, other_tok, gown, gain_own, gain_other, *rest
):
    outs, gtok_hbm, gtok_other_hbm, proj_hbm = rest[:4], *rest[4:7]
    gtok_other, part, stage, out, sems, g_sems = rest[7:]
    moves = [pltpu.make_async_copy(gtok, gtok_hbm, g_sems.at[0])]
    moves[0].start()
    for slot, (weights, mine, theirs) in enumerate(((left, own_x, other_x), (right, own_y, other_y))):
        at = pl.ds(slot * HALF, HALF)
        gtok_other[:, at] = dot(gother[...], weights[...], ((1,), (0,))).astype(BF)
        moves.append(pltpu.make_async_copy(gtok_other.at[:, at], gtok_other_hbm.at[:, at], g_sems.at[1 + slot]))
        moves[-1].start()
        part[slot] = (
            dot(mine[...], gtok[:, at], ((1,), (0,))) + dot(theirs[...], gtok_other[:, at], ((1,), (0,)))
        ).astype(BF)
        for half in range(2):
            rows = part.at[slot, pl.ds(half * HROWS, HROWS)]
            moves.append(pltpu.make_async_copy(rows, outs[2 * slot + half], sems.at[slot, half]))
            moves[-1].start()
    gain = split_gain(gain_own[0:1] + gain_other[0:1]).astype(BF)
    for x in range(4):
        rows = slice(x * XPROJ, (x + 1) * XPROJ)
        share = dot(own_tok[rows, :], gown[...], ((1,), (0,))) + dot(other_tok[rows, :], gother[...], ((1,), (0,)))
        for y in range(4):
            for z in range(4):
                stage[z, y * 32 + x * 8 : y * 32 + x * 8 + 8, :] = share[y * 32 + z * 8 : y * 32 + z * 8 + 8]
    for z in range(4):
        out[z, 0:128, :] = stage[z].astype(BF)
        out[z, 128:144, :] = gain
        moves.append(pltpu.make_async_copy(out.at[z], proj_hbm.at[z], g_sems.at[3 + z]))
        moves[-1].start()
    for copy in moves:
        copy.wait()


def conv_first(gtok, gother, left, right, blocks, grads, gain, gain_other):
    return pl.pallas_call(
        conv_first_kernel,
        in_specs=[VMEM_SPEC] * 13,
        out_specs=[HBM_SPEC] * 7,
        out_shape=[pltpu.HBM((HROWS, HALF), BF)] * 4
        + [pltpu.HBM((512, COUT), BF)] * 2
        + [pltpu.HBM((4, 144, DM), BF)],
        scratch_shapes=[
            pltpu.VMEM((512, COUT), BF),
            pltpu.VMEM((2, XCONV, HALF), BF),
            pltpu.VMEM((4, XPROJ, DM), F32),
            pltpu.VMEM((4, 144, DM), BF),
            pltpu.SemaphoreType.DMA((2, 2)),
            pltpu.SemaphoreType.DMA((7,)),
        ],
        compiler_params=pltpu.CompilerParams(vmem_limit_bytes=24 << 20),
        cost_estimate=pl.CostEstimate(flops=4_000_000_000, bytes_accessed=8_000_000, transcendentals=0),
        name="conv_first",
    )(gtok, gother, left, right, *blocks, grads, gain, gain_other)


def conv_second_kernel(pos_ref, own_hbm, other_hbm, gtok_hbm, gtok_other_hbm, after, *rest):
    outs, own, other, gtok, gtok_other, part, sems, in_sems, g_sems = rest[:6], *rest[6:]
    grads = [
        pltpu.make_async_copy(gtok_hbm, gtok, g_sems.at[0]),
        pltpu.make_async_copy(gtok_other_hbm, gtok_other, g_sems.at[1]),
    ]
    blocks = []
    for s in (1, 3, 0, 2):
        x = (pos_ref[0] + s) & 3
        rows = pl.ds(pl.multiple_of(x * XCONV, 64), XCONV)
        blocks.append(
            [
                pltpu.make_async_copy(hbm.at[rows], vmem.at[x], in_sems.at[i, s])
                for i, (hbm, vmem) in enumerate(((own_hbm, own), (other_hbm, other)))
            ]
        )
    for copy in (grads[0], blocks[0][0], grads[1], blocks[0][1], *blocks[1], *blocks[2], *blocks[3]):
        copy.start()
    sends = []
    for axis in (0, 2):
        for s in (1, 3, 0):
            slot = len(sends)
            if slot == 0:
                for copy in grads:
                    copy.wait()
            for block in {0: blocks[:1], 1: blocks[1:2], 2: blocks[2:3], 3: blocks[3:]}.get(slot, []):
                for copy in block:
                    copy.wait()
            at = pl.ds(axis * HALF // 2, HALF)
            part[slot] = (
                dot(by_turn(axis, pos_ref, s, own), gtok[:, at], ((1,), (0,)))
                + dot(by_turn(axis, pos_ref, s, other), gtok_other[:, at], ((1,), (0,)))
            ).astype(BF)
            sends.append(pltpu.make_async_copy(part.at[slot], outs[slot], sems.at[slot]))
            sends[-1].start()
    for copy in sends:
        copy.wait()


def conv_second(pos, own, other, gtok, gtok_other, after):
    return pl.pallas_call(
        conv_second_kernel,
        in_specs=[SMEM_SPEC] + [HBM_SPEC] * 5,
        out_specs=[HBM_SPEC] * 6,
        out_shape=[pltpu.HBM((XCONV, HALF), BF)] * 6,
        scratch_shapes=[
            pltpu.VMEM((NX, XCONV, 512), BF),
            pltpu.VMEM((NX, XCONV, 512), BF),
            pltpu.VMEM((512, COUT), BF),
            pltpu.VMEM((512, COUT), BF),
            pltpu.VMEM((6, XCONV, HALF), BF),
            pltpu.SemaphoreType.DMA((6,)),
            pltpu.SemaphoreType.DMA((2, 4)),
            pltpu.SemaphoreType.DMA((2,)),
        ],
        compiler_params=pltpu.CompilerParams(vmem_limit_bytes=24 << 20),
        cost_estimate=pl.CostEstimate(flops=COST_SECOND, bytes_accessed=3_000_000, transcendentals=0),
        name="conv_second",
    )(pos, *[in_hbm(a) for a in (own, other, gtok, gtok_other, after)])


def add_kernel(ahead_in, behind_in, from_behind, from_ahead, ahead, behind, part, sems):
    halves = (
        (ahead_in, ahead, pl.ds(0, HROWS), from_behind),
        (behind_in, behind, pl.ds(HROWS, HROWS), from_ahead),
    )
    loads = [
        pltpu.make_async_copy(old.at[rows], part.at[i], sems.at[0, i]) for i, (old, _, rows, _) in enumerate(halves)
    ]
    stores = [
        pltpu.make_async_copy(part.at[i], new.at[rows], sems.at[1, i]) for i, (_, new, rows, _) in enumerate(halves)
    ]
    for copy in loads:
        copy.start()
    for i in range(2):
        loads[i].wait()
        part[i] = (part[i].astype(F32) + halves[i][3][...].astype(F32)).astype(BF)
        stores[i].start()
    for copy in stores:
        copy.wait()


def relay(axis, halves, ahead, behind, here):
    forward, back = [(i, (i + 1) % 4) for i in range(4)], [(i, (i + 3) % 4) for i in range(4)]
    from_behind = lax.ppermute(halves[0], axis, forward)
    from_ahead = lax.ppermute(halves[1], axis, back)

    def finish():
        one, other = pl.pallas_call(
            add_kernel,
            in_specs=[HBM_SPEC, HBM_SPEC, VMEM_SPEC, VMEM_SPEC],
            out_specs=[HBM_SPEC] * 2,
            out_shape=[pltpu.HBM((XCONV, HALF), BF)] * 2,
            input_output_aliases={0: 0, 1: 1},
            scratch_shapes=[pltpu.VMEM((2, HROWS, HALF), BF), pltpu.SemaphoreType.DMA((2, 2))],
            compiler_params=pltpu.CompilerParams(vmem_limit_bytes=16 << 20),
            cost_estimate=pl.CostEstimate(flops=COST_ADD, bytes_accessed=3_000_000, transcendentals=0),
            name="add_" + axis,
        )(in_hbm(ahead), in_hbm(behind), from_behind, from_ahead)
        return [here, lax.ppermute(one, axis, forward), lax.ppermute(other, axis, back)]

    return finish()


def split_gain(gain):
    high = gain.astype(BF).astype(F32)
    rest = gain - high
    low = rest.astype(BF).astype(F32)
    return jnp.concatenate(
        [
            jnp.broadcast_to(high, (8, DM)),
            jnp.broadcast_to(low, (8, DM)),
        ],
        axis=0,
    )


def small(kernel, name, outs, args, scratch=(), mib=16, flops=1_000_000, after=()):
    bytes_in = sum(a.size * a.dtype.itemsize for a in args)
    return pl.pallas_call(
        kernel,
        in_specs=[SMEM_SPEC] + [VMEM_SPEC] * (len(args) - 1) + [ANY_SPEC] * len(after),
        out_specs=[VMEM_SPEC] * len(outs),
        out_shape=[jax.ShapeDtypeStruct(*o) for o in outs],
        scratch_shapes=list(scratch),
        compiler_params=pltpu.CompilerParams(vmem_limit_bytes=mib << 20),
        cost_estimate=pl.CostEstimate(flops=flops, bytes_accessed=bytes_in, transcendentals=0),
        name=name,
    )(*args, *after)


def first_sum_kernel(pos_ref, a, b, c, *outs):
    for s, ref in enumerate(outs):
        at = pl.ds(pl.multiple_of(((pos_ref[2] + s) & 3) * YROWS, 16), YROWS)
        ref[...] = (a[at, :].astype(F32) + (b[at, :].astype(F32) + c[at, :].astype(F32))).astype(BF)


def sum_four(ref, rows, gain_rows):
    got = [ref[i, 0:rows, :].astype(F32) for i in range(4)]
    high, low = pl.ds(gain_rows, 8), pl.ds(gain_rows + 8, 8)
    gains = [ref[i, high, :].astype(F32) + ref[i, low, :].astype(F32) for i in range(4)]
    gain = split_gain(((gains[0] + gains[1]) + (gains[2] + gains[3]))[0:1])
    return (got[0] + got[1]) + (got[2] + got[3]), gain


def proj_sum_kernel(pos_ref, got_ref, out_ref, gains):
    total, gain = sum_four(got_ref, 128, 128)
    gains[...] = jnp.zeros_like(gains)
    for t in range(DM // 128):
        piece = slice(128 * t, 128 * t + 128)
        gains[t : t + 1, 0:128] = gain[0:1, piece]
        gains[t : t + 1, 128:256] = gain[8:9, piece]
    for k in range(16):
        rows = total[8 * k : 8 * k + 8]
        halves = jnp.concatenate([rows[:, : DM // 2], rows[:, DM // 2 :]], axis=0)
        out_ref[k] = jnp.concatenate([halves, gains[...]], axis=1).astype(BF)


def second_sum_kernel(pos_ref, a, b, c, o0, o1, o2, o3, part, by_z):
    part[...] = a[...].astype(F32) + (b[...].astype(F32) + c[...].astype(F32))
    for x in range(4):
        for z in range(4):
            at = x * YROWS + z * CONV_ROWS
            by_z[z, x * CONV_ROWS : (x + 1) * CONV_ROWS, :] = part[at : at + CONV_ROWS, :]
    for s, ref in enumerate((o0, o1, o2, o3)):
        ref[...] = by_z[(pos_ref[3] + s) & 3].astype(BF)


def plane_sum_kernel(along, pos_ref, a, b, c, d, o0, o1, o2, o3, part, split):
    part[...] = (a[...].astype(F32) + b[...].astype(F32)) + (c[...].astype(F32) + d[...].astype(F32))
    for i in range(4):
        split[i, 0:CONV_ROWS, :] = part[CONV_ROWS * i : CONV_ROWS * (i + 1), :]
    for s, ref in enumerate((o0, o1, o2, o3)):
        ref[...] = split[(pos_ref[along] + s) & 3, 0:CONV_ROWS, :].astype(BF)


def conv_total_kernel(pos_ref, a0, a1, a2, a3, b0, b1, b2, b3, after, out_ref):
    for at, refs in ((0, (a0, a1, a2, a3)), (HALF, (b0, b1, b2, b3))):
        p, q, r, t = [ref[...].astype(F32) for ref in refs]
        out_ref[:, at : at + HALF] = (p + q) + (r + t)


def proj_total_kernel(pos_ref, got_ref, out_ref, gain_ref):
    total = got_ref[0].astype(F32)
    for i in range(1, 16):
        total = total + got_ref[i].astype(F32)
    out_ref[:, : DM // 2] = total[0:8, : DM // 2]
    out_ref[:, DM // 2 :] = total[8:16, : DM // 2]
    gains = total[:, DM // 2 : DM // 2 + 128] + total[:, DM // 2 + 128 :]
    for t in range(DM // 128):
        gain_ref[:, 128 * t : 128 * t + 128] = gains[t : t + 1]


def turn(axis, parts):
    return [parts[0]] + [
        lax.ppermute(parts[s], axis, [(i, (i + s) % 4) for i in range(4)]) for s in (1, 2, 3)
    ]


def per_device(pre_conv, conv_weight, proj_weight, norm_gain, slab_cotangent, page_tiles, block_dest):
    pos = jnp.stack([lax.axis_index(axis) for axis in ALL]).astype(jnp.int32)
    swap = functools.partial(lax.ppermute, axis_name="core", perm=[(0, 1), (1, 0)])
    cot = lax.all_to_all(slab_cotangent.reshape(16, 64, DM), ("y", "z"), 0, 0, tiled=True)
    own, other, values, proj_t = forward(
        pos, page_tiles, pre_conv.reshape(2048, CIN), conv_weight, proj_weight
    )
    other = swap(other)
    grads, gain, left = norm(block_dest[:, 0], cot, values, norm_gain.reshape(1, DM), proj_t)
    gother, gain_other = swap(grads), swap(gain)

    gtok, right, *blocks = token_grad(pos, grads, left, proj_t, own, other)
    *halves, gtok, gtok_far, proj = conv_first(gtok, gother, left, right, blocks, grads, gain, gain_other)
    shares = conv_second(pos, own, other, gtok, gtok_far, proj)
    proj = lax.all_to_all(proj, "z", 0, 0, tiled=True)
    first = relay("x", halves[:2], *shares[:3])
    second = relay("y", halves[2:], *shares[3:])

    plane = ((YROWS, HALF), BF)
    (proj,) = small(proj_sum_kernel, "proj_sum", [((16, 16, DM // 2 + 256), BF)], [pos, proj], [pltpu.VMEM((16, 256), F32)])
    first = turn("y", small(first_sum_kernel, "first_sum", [plane] * 4, [pos, *first], flops=COST_SUM))
    second = small(
        second_sum_kernel,
        "second_sum",
        [plane] * 4,
        [pos, *second],
        [pltpu.VMEM((XCONV, HALF), F32), pltpu.VMEM((4, YROWS, HALF), F32)],
        flops=COST_SUM,
    )
    second = turn("z", second)
    proj = lax.all_to_all(proj, ("y", "x"), 0, 0, tiled=True)
    grad_proj, grad_gain = small(
        proj_total_kernel, "proj_total", [((PROJ_ROWS, DM), F32), ((1, DM), F32)], [pos, proj]
    )
    lines = ((CONV_ROWS, HALF), BF)
    scratch = [pltpu.VMEM((YROWS, HALF), F32), pltpu.VMEM((4, 40, HALF), F32)]
    second = small(
        functools.partial(plane_sum_kernel, 0), "plane_sum_x", [lines] * 4, [pos, *second], scratch, flops=COST_SUM
    )
    first = small(
        functools.partial(plane_sum_kernel, 3), "plane_sum_z", [lines] * 4, [pos, *first], scratch, flops=COST_SUM
    )
    (grad_conv,) = small(
        conv_total_kernel,
        "conv_total",
        [((CONV_ROWS, COUT), F32)],
        [pos, *turn("z", first), *turn("x", second)],
        flops=COST_SUM,
        after=[grad_gain],
    )
    return grad_conv, grad_proj, grad_gain.reshape(DM)


def solution(mesh):
    split = Mesh(mesh.devices.reshape(4, 2, 4, 4), ALL)
    return jax.shard_map(
        per_device,
        mesh=split,
        in_specs=(P(ALL), P(), P(), P(), P(ALL), P(ALL), P(ALL)),
        out_specs=(P(ALL), P(ALL), P()),
        check_vma=False,
    )
```
